128 devices in a mesh: dp: 8 (over x_hi, z), tensor: 16 (over x_lo, y, core).
Axes of the slice: x: 4 (x_hi: 2, x_lo: 2; x = x_hi * 2 + x_lo), y: 4, z: 4, core: 2. Of those that a mesh axis runs over, the one named last changes fastest.
Arguments:
- dense_hidden: bfloat16 [2048, 9216], P('dp', 'tensor'), may hold values from -6 to 6
- dense_down: bfloat16 [9216, 3584], P('tensor', 'dp'), may hold values from -0.0625 to 0.0625
- residual: bfloat16 [2048, 3584], P(('dp', 'tensor')), may hold values from -6 to 6
- norm_gain: bfloat16 [3584], replicated, may hold values from 0.099609375 to 1.8984375
- expert_ids: int32 [2048, 8], P(('dp', 'tensor')), may hold values from 0 to 127, all different within a row; in each aligned block of 16 rows (0 to 15, 16 to 31, ...) at most 2 rows name the same one
- route_weights: float32 [2048, 8], P(('dp', 'tensor')), may hold values from 0.05 to 0.5
- w_gate: bfloat16 [128, 3584, 1024], P(('dp', 'tensor')), may hold values from -0.09375 to 0.09375
- w_up: bfloat16 [128, 3584, 1024], P(('dp', 'tensor')), may hold values from -0.09375 to 0.09375
- w_down: bfloat16 [128, 1024, 3584], P(('dp', 'tensor')), may hold values from -0.1875 to 0.1875
- out_cotangent: bfloat16 [2048, 3584], P(('dp', 'tensor')), may hold values from -6 to 6
Outputs:
- moe_out: bfloat16 [2048, 3584], P(('dp', 'tensor'))
- grad_stream: bfloat16 [2048, 3584], P(('dp', 'tensor'))
- grad_hidden: bfloat16 [2048, 9216], P('dp', 'tensor')
The draws below stay inside these ranges and needn't reach their ends.
Inputs may be any that keep to these rules, and one draw needn't show every extreme that they name: `expert_ids`: each row names 8 different experts. Among the 16 rows of one aligned block no expert is named more than 2 times, a bound that some block reaches.
All inputs are finite; a program needn't handle non-finite values.
Results may differ from the reference program's by a relative error of at most 0.012.
Values may be sent and summed in bfloat16 or wider, within the bound.
A program may use at most 128 MiB of HBM per device.

```python
import math
import jax
import jax.numpy as jnp
import numpy as np
from jax import lax

D = 3584
FF = 9216
FE = 1024
TOP = 8
TOK_DEV = 16
EXPERTS = 128
CAP = 2
TOKENS = 2048


def shard_levels(rng, extent, shards, least, largest):
    gain, own = 1.0, jax.random.fold_in(rng, 6)
    for dim, blocks in shards:
        heights = jnp.exp(jax.random.uniform(jax.random.fold_in(own, dim), (blocks,), jnp.float32, least / len(shards), largest / len(shards)))
        gain = gain * jnp.repeat(heights, extent[dim] // blocks).reshape([-1 if axis == dim else 1 for axis in range(len(extent))])
    return gain


def assign_block(key, own, number, rows, amount, top, bound, lean):
    order = jax.random.permutation(key, amount)
    crowded, ordinary = load_shares(amount, rows * top, bound, lean, True), load_shares(amount, rows * top, bound, lean, False)
    places = jnp.arange(amount)

    def named(sizes, offset_by):
        used = int((sizes > 0).sum())
        fixed = max(1, used // 4)
        passed = fixed + (places - fixed + offset_by * (used - fixed)) % max(1, amount - fixed)
        return jnp.zeros((amount,), jnp.int32).at[order[jnp.where(places < fixed, places, passed)]].set(jnp.asarray(sizes, jnp.int32))

    sizes = jnp.where(number % 4 == 0, named(crowded, number // 4), named(ordinary, number - number // 4 - 1))
    mixed = jax.random.permutation(jax.random.fold_in(own, 3), amount)
    giver, sink = mixed[0:amount // 2 * 2:2], mixed[1:amount // 2 * 2:2]
    slack = jnp.minimum(sizes[giver] - 1, bound - sizes[sink]) // 2
    slack = jnp.where((giver == order[0]) | (sink == order[0]) | (sizes[sink] == 0), 0, jnp.maximum(slack, 0))
    passed = jax.random.randint(jax.random.fold_in(own, 4), (amount // 2,), 0, 1 << 20) % (slack + 1)
    sizes = sizes.at[giver].add(-passed).at[sink].add(passed)
    items = jnp.searchsorted(jnp.cumsum(sizes), jnp.arange(rows * top), side="right").astype(jnp.int32)
    table = items.reshape(top, rows).T
    table = table[jax.random.permutation(jax.random.fold_in(own, 1), rows)]
    offset_by = jax.random.randint(jax.random.fold_in(own, 2), (rows, 1), 0, top)
    return jnp.take_along_axis(table, (jnp.arange(top)[None, :] + offset_by) % top, axis=1)


def load_shares(amount, total, most, slope, full):
    portions = [(1 << 20) // math.isqrt(standing ** slope) + 1 for standing in range(1, amount + 1)]
    largest = most if full else min(most, max(-(-total // amount), total * portions[0] // sum(portions)))
    least = 1 if total - largest >= amount - 1 else 0
    given, surplus = [largest] + [least] * (amount - 1), total - largest - least * (amount - 1)
    while surplus > 0:
        movable = [i for i in range(1, amount) if given[i] < largest] or [i for i in range(1, amount) if given[i] < most]
        mass, remaining = sum([portions[i] for i in movable]), surplus
        for i in movable:
            addition = min(most - given[i], max(1, remaining * portions[i] // mass), surplus)
            given[i] = given[i] + addition
            surplus = surplus - addition
    return np.array(given)


def noise(stream_key, shape, spread, reach, split=(), kind=jnp.bfloat16):
    entries = jax.random.normal(stream_key, shape, jnp.float32) * spread
    if len(split) > 0:
        entries = shard_levels(stream_key, shape, split, -0.22, 0.18) * entries
    return jnp.clip(entries, min=-reach, max=reach).astype(kind)


def setup_inputs(seed: int = 0) -> dict:
    splits = jax.random.split(jax.random.key(seed), 11)
    dense_hidden = noise(splits[0], (TOKENS, FF), 1.0, 6.0, ((0, 8), (1, 16)))
    dense_down = noise(splits[1], (FF, D), FF ** -0.5, 0.0625, ((0, 16), (1, 8)))
    residual = noise(splits[2], (TOKENS, D), 1.0, 6.0, ((0, 128),))
    norm_gain = jnp.clip(1.0 + 0.18 * jax.random.normal(splits[3], (D,), jnp.float32), 0.099609375, 1.8984375).astype(jnp.bfloat16)
    expert_ids_keys = jax.random.split(jax.random.fold_in(splits[4], 1), TOKENS // TOK_DEV)
    expert_ids_turns = jax.random.permutation(jax.random.fold_in(splits[4], 3), TOKENS // TOK_DEV)
    expert_ids = jax.vmap(lambda own, number: assign_block(jax.random.fold_in(splits[4], 2), own, number, TOK_DEV, EXPERTS, TOP, CAP, 2))(expert_ids_keys, expert_ids_turns).reshape((TOKENS, TOP))
    route_weights = jnp.clip(jnp.exp(math.log(0.5) - 2.3025851 * jax.random.uniform(splits[5], (TOKENS, TOP), jnp.float32) ** shard_levels(splits[5], (TOKENS, TOP), ((0, 128),), -0.2, 0.2)), 0.05, 0.5)
    w_gate = noise(splits[6], (EXPERTS, D, FE), D ** -0.5, 0.09375, ((0, 128),))
    w_up = noise(splits[7], (EXPERTS, D, FE), D ** -0.5, 0.09375, ((0, 128),))
    w_down = noise(splits[8], (EXPERTS, FE, D), FE ** -0.5, 0.1875, ((0, 128),))
    out_cotangent = noise(splits[9], (TOKENS, D), 1.0, 6.0, ((0, 128),))
    return dict(dense_hidden=dense_hidden, dense_down=dense_down, residual=residual, norm_gain=norm_gain, expert_ids=expert_ids, route_weights=route_weights, w_gate=w_gate, w_up=w_up, w_down=w_down, out_cotangent=out_cotangent)


def slot_table(expert_ids):
    tok_total = expert_ids.shape[0]
    blocks = tok_total // TOK_DEV
    onehot = (expert_ids[:, :, None] == jnp.arange(EXPERTS, dtype=jnp.int32)[None, None, :]).astype(jnp.int32)
    flat_hot = onehot.reshape(blocks, TOK_DEV * TOP, EXPERTS)
    running = jnp.cumsum(flat_hot, axis=1) - flat_hot
    return lax.optimization_barrier(jnp.sum(running * flat_hot, axis=2)).reshape(tok_total, TOP).astype(jnp.int32)

def reference(dense_hidden, dense_down, residual, norm_gain, expert_ids, route_weights, w_gate, w_up, w_down, out_cotangent):
    tok_total = residual.shape[0]
    model_width = residual.shape[1]
    dense_out = jnp.dot(dense_hidden, dense_down, preferred_element_type=jnp.float32)
    stream = (residual.astype(jnp.float32) + dense_out).astype(jnp.bfloat16)
    stream_f = stream.astype(jnp.float32)
    inverse = lax.rsqrt(lax.optimization_barrier(jnp.mean(stream_f * stream_f, axis=-1, keepdims=True)) + 1e-06)
    gain_f = norm_gain.astype(jnp.float32)
    normed = (stream_f * inverse * gain_f).astype(jnp.bfloat16)
    slot_index = slot_table(expert_ids)
    source = (jnp.arange(tok_total, dtype=jnp.int32) // TOK_DEV)[:, None]
    position = (source * CAP + slot_index).astype(jnp.int32)
    slot_rows = EXPERTS * CAP
    token_index = jnp.broadcast_to(jnp.arange(tok_total, dtype=jnp.int32)[:, None], (tok_total, TOP))
    route_table = jnp.full((EXPERTS, slot_rows), tok_total, jnp.int32).at[expert_ids, position].set(token_index)
    padded_in = jnp.concatenate([normed, jnp.zeros((1, model_width), jnp.bfloat16)], axis=0)

    def forward_expert(packed):
        row_index, gate_w, up_w, down_w = packed
        expert_rows = padded_in[row_index]
        gate_pre = jnp.dot(expert_rows, gate_w, preferred_element_type=jnp.float32)
        up_pre = jnp.dot(expert_rows, up_w, preferred_element_type=jnp.float32)
        act = (jax.nn.silu(gate_pre) * up_pre).astype(jnp.bfloat16)
        expert_out = jnp.dot(act, down_w, preferred_element_type=jnp.float32).astype(jnp.bfloat16)
        return (expert_out, gate_pre, up_pre)
    expert_out, gate_all, up_all = lax.map(forward_expert, (route_table, w_gate, w_up, w_down))
    picked = expert_out[expert_ids, position].astype(jnp.float32)
    moe_out = (stream_f + lax.optimization_barrier(jnp.sum(route_weights[:, :, None] * picked, axis=1))).astype(jnp.bfloat16)
    cotangent = out_cotangent.astype(jnp.float32)
    grad_rows = (route_weights[:, :, None] * cotangent[:, None, :]).astype(jnp.bfloat16)
    grad_send = jnp.zeros((EXPERTS, slot_rows, model_width), jnp.bfloat16).at[expert_ids, position].set(grad_rows)
    contract = (((1,), (1,)), ((), ()))

    def backward_expert(packed):
        grad_arrived, gate_pre, up_pre, gate_w, up_w, down_w = packed
        grad_act = lax.dot_general(grad_arrived, down_w, contract, preferred_element_type=jnp.float32)
        sigmoid_g = jax.nn.sigmoid(gate_pre)
        silu_gate = gate_pre * sigmoid_g
        grad_gate = (grad_act * up_pre * sigmoid_g * (1.0 + gate_pre * (1.0 - sigmoid_g))).astype(jnp.bfloat16)
        grad_up = (grad_act * silu_gate).astype(jnp.bfloat16)
        returned = lax.dot_general(grad_gate, gate_w, contract, preferred_element_type=jnp.float32)
        returned = returned + lax.dot_general(grad_up, up_w, contract, preferred_element_type=jnp.float32)
        return returned.astype(jnp.bfloat16)
    grad_back = lax.map(backward_expert, (grad_send, gate_all, up_all, w_gate, w_up, w_down))
    grad_normed = lax.optimization_barrier(jnp.sum(grad_back[expert_ids, position].astype(jnp.float32), axis=1))
    unit = stream_f * inverse
    scaled = grad_normed * gain_f
    grad_f = cotangent + inverse * (scaled - unit * lax.optimization_barrier(jnp.mean(scaled * unit, axis=-1, keepdims=True)))
    grad_stream = grad_f.astype(jnp.bfloat16)
    grad_hidden = lax.dot_general(grad_stream, dense_down, contract, preferred_element_type=jnp.float32).astype(jnp.bfloat16)
    return (moe_out, grad_stream, grad_hidden)
```

```python
import jax
import jax.numpy as jnp
from jax import lax
from jax.experimental import pallas as pl
from jax.experimental.pallas import tpu as pltpu
from jax.sharding import PartitionSpec as P

MESH = pl.DeviceIdType.MESH
BF = jnp.bfloat16
F32 = jnp.float32
CHIPS = 64
ROWS = 16
NT = (((1,), (1,)), ((), ()))


def mm(a, b):
    return jnp.dot(a, b, preferred_element_type=F32)


def mm_t(a, b):
    return lax.dot_general(a, b, NT, preferred_element_type=F32)


def landed(ref, sem):
    pltpu.make_async_copy(ref, ref, sem).wait()


def kernel(
    hid_h, down_h, res, gain, cot, key_in, wt_in, wg_h, wu_h, wd_h,
    moe_o, gs_o, gh_o,
    hid, down, wg, wu, wd,
    cot2, key2, wt2, nrm2,
    m01, mg, c01, cw, perm, perm_t, cn, cg,
    buf_a, garr, buf_b, narr, hret, eret,
    xin, gact, act, gg, gu, zin,
    pf, psend, prec, rs_send, rs_recv, stream,
    acc, pax, prx, gs_all,
    loc, ex_s, ex_r, ag_s, ag_r, ps_s, ps_r, rs_s, rs_r,
    ga_s, ga_r, na_s, na_r, ha_s, ha_r, ea_s, ea_r, px_s, px_r, gs_s, gs_r, fw_s, fw_r,
):
    width = res.shape[1]
    quarter = width // 4
    half = quarter // 2
    dp = lax.axis_index("dp")
    tn = lax.axis_index("tensor")
    c = tn % 2
    tc = tn // 2
    chip = dp * 8 + tc
    z, y = dp % 4, tc % 4
    x = (dp // 4) * 2 + tc // 4
    partner = (dp, tc * 2 + 1 - c)

    def peer(i):
        x2 = (x + i % 4) % 4
        y2 = (y + (i // 4) % 4) % 4
        z2 = (z + i // 16) % 4
        return (x2 // 2) * 4 + z2, (x2 % 2) * 4 + y2

    def send(src, dst, s_sem, r_sem, device):
        copy = pltpu.make_async_remote_copy(
            src_ref=src, dst_ref=dst, send_sem=s_sem, recv_sem=r_sem,
            device_id=device, device_id_type=MESH,
        )
        copy.start()
        return copy

    pltpu.make_async_copy(down_h, down.at[dp], ag_r.at[dp]).start()
    load_hid = pltpu.make_async_copy(hid_h, hid, loc.at[0])
    load_hid.start()
    load_wd = pltpu.make_async_copy(wd_h, wd, loc.at[1])
    load_wg = pltpu.make_async_copy(wg_h, wg, loc.at[2])
    load_wu = pltpu.make_async_copy(wu_h, wu, loc.at[3])
    load_wd.start()
    load_wg.start()
    load_wu.start()

    barrier = pltpu.get_barrier_semaphore()

    def greet(i, carry):
        d2, t2 = peer(i)
        pl.semaphore_signal(barrier, inc=1, device_id=(d2, t2 * 2 + c), device_id_type=MESH)
        return carry

    lax.fori_loop(1, CHIPS, greet, 0)
    pl.semaphore_signal(barrier, inc=1, device_id=partner, device_id_type=MESH)
    pl.semaphore_wait(barrier, CHIPS)

    ex = [
        send(cot, cot2.at[c], ex_s.at[0], ex_r.at[0], partner),
        send(key_in, key2.at[c], ex_s.at[1], ex_r.at[1], partner),
        send(wt_in, wt2.at[c], ex_s.at[2], ex_r.at[2], partner),
    ]
    cot2[c] = cot[...]
    key2[c] = key_in[...]
    wt2[c] = wt_in[...]

    def gather_down(i, carry):
        d2 = ((dp // 4 + i // 4) % 2) * 4 + (z + i % 4) % 4
        send(down_h, down.at[dp], ag_s.at[i], ag_r.at[dp], (d2, tn))
        return carry

    lax.fori_loop(1, 8, gather_down, 0)

    o = lax.broadcasted_iota(jnp.int32, (256, 256), 0)
    i = lax.broadcasted_iota(jnp.int32, (256, 256), 1)
    perm[...] = jnp.where((o % 64) // 4 * 16 + o // 64 * 4 + o % 4 == i, 1.0, 0.0).astype(BF)
    perm_t[...] = jnp.where((i % 64) // 4 * 16 + i // 64 * 4 + i % 4 == o, 1.0, 0.0).astype(BF)

    for e in ex:
        e.wait_recv()

    def place(n, carry):
        r0 = pl.multiple_of(n * 128, 128)
        r = r0 + lax.broadcasted_iota(jnp.int32, (128, 128), 0)
        lane = lax.broadcasted_iota(jnp.int32, (128, 128), 1)
        want = jnp.where((r // 4) % 4 == lane // 32, (r // 16) * 8 + 4 * c + r % 4, -1)
        lane1 = lax.broadcasted_iota(jnp.int32, (8, 128), 1)
        first = (lane1 // 16) % 2 == 0
        keys = jnp.where(first, key2[0], key2[1])
        wts = jnp.where(first, wt2[0], wt2[1])
        one = jnp.zeros((128, 128), F32)
        wsum = jnp.zeros((128, 128), F32)
        for k in range(8):
            hit = want == keys[k : k + 1, :]
            one = jnp.where(hit, 1.0, one)
            wsum = jnp.where(hit, wts[k : k + 1, :], wsum)
        hi = wsum.astype(BF)
        lo = (wsum - hi.astype(F32)).astype(BF)
        m01[pl.ds(r0, 128), :] = one.astype(BF)
        mg[pl.ds(r0, 128), 0:128] = hi
        mg[pl.ds(r0, 128), 128:256] = lo
        one_t = jnp.transpose(one)
        w_t = jnp.transpose(wsum)
        hi_t = w_t.astype(BF)
        c01[:, pl.ds(r0, 128)] = one_t.astype(BF)
        cw[0:128, pl.ds(r0, 128)] = hi_t
        cw[128:256, pl.ds(r0, 128)] = (w_t - hi_t.astype(F32)).astype(BF)
        return carry

    lax.fori_loop(0, 8, place, 0)

    def scatter_units(src, dst, s_sem, r_sem):
        def one(i, carry):
            d2, t2 = peer(i)
            send(src.at[d2 * 8 + t2], dst.at[chip], s_sem, r_sem.at[chip // 16], (d2, t2 * 2 + c))
            return carry

        lax.fori_loop(1, CHIPS, one, 0)
        pltpu.make_async_copy(src.at[chip], dst.at[chip], r_sem.at[chip // 16]).start()

    def sent_units(src, s_sem):
        landed(src.at[pl.ds(0, CHIPS - 1)], s_sem)

    for q in range(4):
        for b in range(2):
            part = cot2[b, :, q * quarter : (q + 1) * quarter]
            row = q * 32 + b * 16
            cg[row : row + 16, :] = part
            cg[128 + row : 128 + row + 16, :] = part

    def place_cot(g, carry):
        rows = mm(mg[pl.ds(pl.multiple_of(g * 256, 256), 256), :], cg[...])
        buf_a[pl.ds(g * 16, 16)] = rows.astype(BF).reshape(16, ROWS, quarter)
        return carry

    lax.fori_loop(0, 4, place_cot, 0)
    scatter_units(buf_a, garr, ga_s, ga_r)

    load_hid.wait()

    def dense(i, carry):
        m = (dp // 2 + i) % 4
        for h in range(2):
            landed(down.at[2 * m + h], ag_r.at[2 * m + h])
            p = mm(hid[...], down[2 * m + h])
            pf[m, :, :, h * half : (h + 1) * half] = p.reshape(16, 16, half)

        def pack(t, carry):
            psend[m, t] = pf[m, 2 * t + 1 - c].astype(BF)
            return carry

        lax.fori_loop(0, 8, pack, 0)
        send(psend.at[m], prec.at[m], ps_s.at[m], ps_r.at[m], partner)
        return carry

    lax.fori_loop(0, 4, dense, 0)

    def reduce(i, carry):
        m = (dp // 2 + i) % 4
        landed(prec.at[m], ps_r.at[m])

        def add(t, carry):
            rs_send[m, t] = (pf[m, 2 * t + c] + prec[m, t].astype(F32)).astype(BF)
            return carry

        lax.fori_loop(0, 8, add, 0)

        def out(k, carry):
            t2 = ((tc // 4 + k // 4) % 2) * 4 + (y + k % 4) % 4
            send(rs_send.at[m, t2], rs_recv.at[m, tc], rs_s.at[m], rs_r.at[m], (dp, t2 * 2 + c))
            return carry

        lax.fori_loop(1, 8, out, 0)
        pltpu.make_async_copy(rs_send.at[m, tc], rs_recv.at[m, tc], rs_r.at[m]).start()
        return carry

    lax.fori_loop(0, 4, reduce, 0)

    square = jnp.zeros((16, 1), F32)
    for m in range(4):
        cols = slice(m * quarter, (m + 1) * quarter)
        landed(rs_recv.at[m], rs_r.at[m])
        total = rs_recv[m, 0].astype(F32)
        for t in range(1, 8):
            total = total + rs_recv[m, t].astype(F32)
        st = (res[:, cols].astype(F32) + total).astype(BF)
        stream[:, cols] = st
        st = st.astype(F32)
        square = square + jnp.sum(st * st, axis=1, keepdims=True)
    inverse = lax.rsqrt(square / width + 1e-6)
    nrm2[c] = (stream[...].astype(F32) * inverse * gain[...].astype(F32)).astype(BF)
    nx = send(nrm2.at[c], nrm2.at[c], ex_s.at[3], ex_r.at[3], partner)
    nx.wait_recv()

    for q in range(4):
        for b in range(2):
            row = q * 32 + b * 16
            cn[row : row + 16, :] = nrm2[b, :, q * quarter : (q + 1) * quarter]

    def place_nrm(g, carry):
        rows = mm(m01[pl.ds(pl.multiple_of(g * 256, 256), 256), :], cn[...])
        buf_b[pl.ds(g * 16, 16)] = rows.astype(BF).reshape(16, ROWS, quarter)
        return carry

    lax.fori_loop(0, 4, place_nrm, 0)
    scatter_units(buf_b, narr, na_s, na_r)

    def collect(arr, r_sem):
        def group(g, carry):
            landed(arr.at[pl.ds(g * 16, 16)], r_sem.at[g])
            rows = mm(perm[...], arr[pl.ds(g * 16, 16)].reshape(256, quarter)).astype(BF)
            for q in range(4):
                xin[pl.ds(pl.multiple_of(g * 64, 64), 64), q * quarter : (q + 1) * quarter] = rows[
                    q * 64 : (q + 1) * 64
                ]
            return carry

        lax.fori_loop(0, 4, group, 0)

    collect(garr, ga_r)
    load_wd.wait()

    def back_down(n, carry):
        at = pl.ds(pl.multiple_of(n * 256, 256), 256)
        gact[:, at] = mm_t(xin[...], wd[at, :])
        return carry

    lax.fori_loop(0, 4, back_down, 0)

    collect(narr, na_r)
    load_wg.wait()
    load_wu.wait()

    def forward(n, carry):
        at = pl.ds(pl.multiple_of(n * 256, 256), 256)
        gate = mm(xin[...], wg[:, at])
        up = mm(xin[...], wu[:, at])
        ga = gact[:, at]
        s = jax.nn.sigmoid(gate)
        silu = gate * s
        act[:, at] = (silu * up).astype(BF)
        gg[:, at] = (ga * up * s * (1.0 + gate * (1.0 - s))).astype(BF)
        gu[:, at] = (ga * silu).astype(BF)
        return carry

    lax.fori_loop(0, 4, forward, 0)

    def to_zin(q, rows):
        rows = rows.astype(BF)
        for g in range(4):
            zin[g, pl.ds(pl.multiple_of(q * 64, 64), 64), :] = rows[g * 64 : (g + 1) * 64]

    def back_in(q, carry):
        at = pl.ds(pl.multiple_of(q * quarter, 128), quarter)
        to_zin(q, mm_t(gg[...], wg[at, :]) + mm_t(gu[...], wu[at, :]))
        return carry

    def from_zin(buf):
        def group(g, carry):
            rows = mm(perm_t[...], zin[g])
            buf[pl.ds(g * 16, 16)] = rows.astype(BF).reshape(16, ROWS, quarter)
            return carry

        lax.fori_loop(0, 4, group, 0)

    lax.fori_loop(0, 4, back_in, 0)
    sent_units(buf_b, na_s)
    from_zin(buf_b)
    scatter_units(buf_b, hret, ha_s, ha_r)

    def down_out(q, carry):
        at = pl.ds(pl.multiple_of(q * quarter, 128), quarter)
        to_zin(q, mm(act[...], wd[:, at]))
        return carry

    lax.fori_loop(0, 4, down_out, 0)
    sent_units(buf_a, ga_s)
    from_zin(buf_a)
    scatter_units(buf_a, eret, ea_s, ea_r)

    def share(u):
        def pack(q, carry):
            pax[u, q] = acc[u, 2 * q + 1 - c]
            return carry

        lax.fori_loop(0, 4, pack, 0)
        return send(pax.at[u], prx.at[u], px_s.at[u], px_r.at[u], partner)

    def summed(u, q):
        return acc[u, 2 * q + c] + prx[u, q]

    total = jnp.zeros((128, quarter), F32)
    for g in range(4):
        landed(hret.at[pl.ds(g * 16, 16)], ha_r.at[g])
        total = total + mm(c01[:, g * 256 : (g + 1) * 256], hret[g * 16 : (g + 1) * 16].reshape(256, quarter))
    acc[0] = total.reshape(8, 16, quarter)
    sh0 = share(0)
    sh0.wait_recv()

    dots = jnp.zeros((16, 1), F32)
    for q in range(4):
        cols = slice(q * quarter, (q + 1) * quarter)
        scaled = summed(0, q) * gain[:, cols].astype(F32)
        dots = dots + jnp.sum(scaled * (stream[:, cols].astype(F32) * inverse), axis=1, keepdims=True)
    mean = dots / width
    for q in range(4):
        cols = slice(q * quarter, (q + 1) * quarter)
        scaled = summed(0, q) * gain[:, cols].astype(F32)
        unit = stream[:, cols].astype(F32) * inverse
        gs_o[:, cols] = (cot[:, cols].astype(F32) + inverse * (scaled - unit * mean)).astype(BF)
    gs_all[tn] = gs_o[...]

    def gather_gs(k, carry):
        t2 = ((tc // 4 + k // 4) % 2) * 4 + (y + k % 4) % 4
        send(gs_all.at[tn], gs_all.at[tn], gs_s.at[k], gs_r.at[tc], (dp, t2 * 2 + c))
        return carry

    lax.fori_loop(1, 8, gather_gs, 0)
    send(gs_all.at[tn], gs_all.at[tn], fw_s.at[tc], fw_r.at[tc], partner)

    def forward_gs(k, carry):
        t2 = ((tc // 4 + k // 4) % 2) * 4 + (y + k % 4) % 4
        b2 = t2 * 2 + c
        landed(gs_all.at[b2], gs_r.at[t2])
        send(gs_all.at[b2], gs_all.at[b2], fw_s.at[t2], fw_r.at[t2], partner)
        return carry

    lax.fori_loop(1, 8, forward_gs, 0)

    def all_gs(t, carry):
        landed(gs_all.at[t * 2 + 1 - c], fw_r.at[t])
        return carry

    lax.fori_loop(0, 8, all_gs, 0)
    rows = gs_all[...].reshape(256, width)
    gh = jnp.zeros(gh_o.shape, F32)
    for j in range(8):
        gh = gh + mm_t(rows[:, j * half : (j + 1) * half], down[j])
    gh_o[...] = gh.astype(BF)

    total = jnp.zeros((256, quarter), F32)
    for g in range(4):
        landed(eret.at[pl.ds(g * 16, 16)], ea_r.at[g])
        total = total + mm(cw[:, g * 256 : (g + 1) * 256], eret[g * 16 : (g + 1) * 16].reshape(256, quarter))
    acc[1] = (total[0:128] + total[128:256]).reshape(8, 16, quarter)
    sh1 = share(1)
    sh1.wait_recv()
    for q in range(4):
        cols = slice(q * quarter, (q + 1) * quarter)
        moe_o[:, cols] = (stream[:, cols].astype(F32) + summed(1, q)).astype(BF)

    for e in ex:
        e.wait_send()
    nx.wait_send()
    sh0.wait_send()
    sh1.wait_send()

    def down_sent(i, carry):
        landed(down_h, ag_s.at[i])
        return carry

    lax.fori_loop(1, 8, down_sent, 0)

    def rest_sent(m, carry):
        landed(psend.at[m], ps_s.at[m])
        landed(rs_send.at[m, pl.ds(0, 7)], rs_s.at[m])
        return carry

    lax.fori_loop(0, 4, rest_sent, 0)
    sent_units(buf_b, ha_s)
    sent_units(buf_a, ea_s)

    def gs_sent(k, carry):
        landed(gs_all.at[0], gs_s.at[k])
        return carry

    lax.fori_loop(1, 8, gs_sent, 0)

    def fw_sent(k, carry):
        landed(gs_all.at[0], fw_s.at[k])
        return carry

    lax.fori_loop(0, 8, fw_sent, 0)


def body(
    dense_hidden, dense_down, residual, norm_gain, expert_ids, route_weights,
    w_gate, w_up, w_down, out_cotangent,
):
    width = residual.shape[1]
    q = width // 4
    hidden_units, cols = dense_down.shape
    fe = w_gate.shape[2]
    core = lax.axis_index("tensor") % 2
    flat = expert_ids.reshape(-1)
    order = jnp.arange(flat.shape[0], dtype=jnp.int32)
    same = (flat[:, None] == flat[None, :]) & (order[None, :] < order[:, None])
    slot = jnp.sum(same.astype(jnp.int32), axis=1).reshape(expert_ids.shape)
    key = jnp.tile((expert_ids * 4 + slot + 2 * core).T, (1, 8))
    wt = jnp.tile(route_weights.T, (1, 8))

    vmem = pl.BlockSpec(memory_space=pltpu.VMEM)
    hbm = pl.BlockSpec(memory_space=pl.ANY)
    V = pltpu.VMEM
    dma = pltpu.SemaphoreType.DMA
    unit = (CHIPS, ROWS, q)
    scratch = [
        V((256, hidden_units), BF), V((8, hidden_units, cols), BF),
        V((width, fe), BF), V((width, fe), BF), V((fe, width), BF),
        V((2, 16, width), BF), V((2, 8, 128), jnp.int32), V((2, 8, 128), F32), V((2, 16, width), BF),
        V((1024, 128), BF), V((1024, 256), BF), V((128, 1024), BF), V((256, 1024), BF),
        V((256, 256), BF), V((256, 256), BF), V((128, q), BF), V((256, q), BF),
        V(unit, BF), V(unit, BF), V(unit, BF), V(unit, BF), V(unit, BF), V(unit, BF),
        V((256, width), BF), V((256, fe), F32), V((256, fe), BF), V((256, fe), BF), V((256, fe), BF),
        V((4, 256, q), BF),
        V((4, 16, 16, q), F32), V((4, 8, 16, q), BF), V((4, 8, 16, q), BF), V((4, 8, 16, q), BF),
        V((4, 8, 16, q), BF), V((16, width), BF),
        V((2, 8, 16, q), F32), V((2, 4, 16, q), F32), V((2, 4, 16, q), F32), V((16, 16, width), BF),
        dma((4,)), dma((4,)), dma((4,)), dma((8,)), dma((8,)), dma((4,)), dma((4,)), dma((4,)), dma((4,)),
        dma, dma((4,)), dma, dma((4,)), dma, dma((4,)), dma, dma((4,)),
        dma((2,)), dma((2,)), dma((8,)), dma((8,)), dma((8,)), dma((8,)),
    ]
    return pl.pallas_call(
        kernel,
        out_shape=(
            jax.ShapeDtypeStruct(residual.shape, BF),
            jax.ShapeDtypeStruct(residual.shape, BF),
            jax.ShapeDtypeStruct(dense_hidden.shape, BF),
        ),
        in_specs=[hbm, hbm, vmem, vmem, vmem, vmem, vmem, hbm, hbm, hbm],
        out_specs=(vmem, vmem, vmem),
        scratch_shapes=scratch,
        compiler_params=pltpu.CompilerParams(
            collective_id=0, has_side_effects=True, vmem_limit_bytes=63 * 1024 * 1024
        ),
    )(
        dense_hidden, dense_down, residual, norm_gain.reshape(1, width), out_cotangent, key, wt,
        w_gate[0], w_up[0], w_down[0],
    )


def solution(mesh):
    rows = P(("dp", "tensor"), None)
    experts = P(("dp", "tensor"), None, None)
    placed = (P("dp", "tensor"), P("tensor", "dp"), rows, P(), rows, rows, experts, experts, experts, rows)
    return jax.shard_map(
        body, mesh=mesh, in_specs=placed, out_specs=(rows, rows, P("dp", "tensor")), check_vma=False
    )
```

```python
import jax
import jax.numpy as jnp
from jax import lax
from jax.experimental import pallas as pl
from jax.experimental.pallas import tpu as pltpu
from jax.sharding import PartitionSpec as P

MESH = pl.DeviceIdType.MESH
BF = jnp.bfloat16
F32 = jnp.float32
CHIPS = 64
EARLY = 24
ROWS = 16
NT = (((1,), (1,)), ((), ()))


def mm(a, b):
    return jnp.dot(a, b, preferred_element_type=F32)


def mm_t(a, b):
    return lax.dot_general(a, b, NT, preferred_element_type=F32)


def landed(ref, sem):
    pltpu.make_async_copy(ref, ref, sem).wait()


def kernel(
    hid_h, down_h, res, gain_in, cot, ids_in, wt_in, wg_h, wu_h, wd_h,
    moe_o, gs_o, gh_o,
    hid, down_t, down2, wg, wu, wd,
    gain, cot2, key2, wt2, nrm2,
    m01, mg, c01, cw, perm, perm_t, cn, cg,
    buf_a, garr, buf_b, narr, hret, eret,
    xin, gact, act, gg, gu, zin,
    pf, psend, prec, rs_send, rs_recv, zxs, zxr, dense_f, stream,
    acc, pax, prx, gsp, gs_all, ghs, ghr,
    loc, ex_s, ex_r, hg_s, hg_r, dg_s, dg_r, zx_s, zx_r, gx_s, gx_r, gh_s, gh_r, ps_s, ps_r, rs_s, rs_r,
    ga_s, ga_r, na_s, na_r, ha_s, ha_r, ea_s, ea_r, px_s, px_r, gs_s, gs_r, fw_s, fw_r,
):
    width = res.shape[1]
    quarter = width // 4
    half = quarter // 2
    dp = lax.axis_index("dp")
    tn = lax.axis_index("tensor")
    c = tn % 2
    tc = tn // 2
    chip = dp * 8 + tc
    z, y = dp % 4, tc % 4
    xh = dp // 4
    x = xh * 2 + tc // 4
    over_x = ((1 - xh) * 4 + z, tn)
    partner = (dp, tc * 2 + 1 - c)

    def peer(i):
        u = i // 4 % 4
        x2 = (x + i) % 4
        y2 = (y + i + u) % 4
        z2 = (z + i + 2 * u + i // 16) % 4
        return (x2 // 2) * 4 + z2, (x2 % 2) * 4 + y2

    def send(src, dst, s_sem, r_sem, device):
        copy = pltpu.make_async_remote_copy(
            src_ref=src, dst_ref=dst, send_sem=s_sem, recv_sem=r_sem,
            device_id=device, device_id_type=MESH,
        )
        copy.start()
        return copy

    pending = []

    def drain():
        for done in pending:
            done()

    def block(h):
        return down_t.at[pl.ds(pl.multiple_of(h * half, 16), half)]

    pltpu.make_async_copy(down_h, block(xh), dg_r.at[xh]).start()
    pltpu.make_async_copy(hid_h, hid.at[z], hg_r.at[z]).start()
    load_wd = pltpu.make_async_copy(wd_h, wd, loc.at[1])
    load_wg = pltpu.make_async_copy(wg_h, wg, loc.at[2])
    load_wu = pltpu.make_async_copy(wu_h, wu, loc.at[3])
    load_wd.start()
    load_wg.start()
    load_wu.start()

    barrier = pltpu.get_barrier_semaphore()

    def greet(i, carry):
        d2, t2 = peer(i)
        pl.semaphore_signal(barrier, inc=1, device_id=(d2, t2 * 2 + c), device_id_type=MESH)
        return carry

    lax.fori_loop(1, CHIPS, greet, 0)
    pl.semaphore_signal(barrier, inc=1, device_id=partner, device_id_type=MESH)

    lane = lax.broadcasted_iota(jnp.int32, (16, 128), 1)
    spread = jnp.where(lane % 16 == lax.broadcasted_iota(jnp.int32, (16, 128), 0), 1.0, 0.0)

    def lanes(a):
        return jnp.dot(a, spread, precision=lax.Precision.HIGHEST, preferred_element_type=F32)

    key2[c] = lanes(ids_in[...].astype(F32))
    wt2[c] = lanes(wt_in[...])
    cot2[c] = cot[...]
    gain[...] = gain_in[...].reshape(1, width)
    pl.semaphore_wait(barrier, CHIPS)

    ex = [
        send(key2.at[c], key2.at[c], ex_s.at[1], ex_r.at[1], partner),
        send(wt2.at[c], wt2.at[c], ex_s.at[2], ex_r.at[2], partner),
        send(cot2.at[c], cot2.at[c], ex_s.at[0], ex_r.at[0], partner),
    ]

    over_z = [(xh * 4 + (z + k) % 4, tn) for k in range(4)]
    for k in (2, 1, 3):
        pending.append(send(hid_h, hid.at[z], hg_s.at[k], hg_r.at[z], over_z[k]).wait_send)
    pending.append(send(down_h, block(xh), dg_s, dg_r.at[xh], over_x).wait_send)

    o = lax.broadcasted_iota(jnp.int32, (256, 256), 0)
    i = lax.broadcasted_iota(jnp.int32, (256, 256), 1)
    perm[...] = jnp.where((o % 64) // 4 * 16 + o // 64 * 4 + o % 4 == i, 1.0, 0.0).astype(BF)
    perm_t[...] = jnp.where((i % 64) // 4 * 16 + i // 64 * 4 + i % 4 == o, 1.0, 0.0).astype(BF)

    pending.extend(e.wait_send for e in ex)
    for e in ex:
        e.wait_recv()

    row = lax.broadcasted_iota(jnp.int32, (128, 128), 0)
    lane = lax.broadcasted_iota(jnp.int32, (128, 128), 1)
    earlier = jnp.where((row // 16 == lane // 16) & (row < lane), 1.0, 0.0).astype(BF)
    first = (lax.broadcasted_iota(jnp.int32, (8, 128), 1) // 16) % 2 == 0
    keys = jnp.where(first, key2[0], key2[1])
    wts = jnp.where(first, wt2[0], wt2[1])

    def place(n, carry):
        r0 = pl.multiple_of(n * 128, 128)
        r = r0 + row
        expert = ((r // 16) * 2 + c).astype(F32)
        member = jnp.zeros((128, 128), F32)
        weight = jnp.zeros((128, 128), F32)
        for k in range(8):
            hit = jnp.abs(keys[k : k + 1, :] - expert) < 0.5
            member = jnp.where(hit, 1.0, member)
            weight = jnp.where(hit, wts[k : k + 1, :], weight)
        slot = mm(member.astype(BF), earlier) + (lane // 16 % 2 * 2).astype(F32)
        here = ((r // 4) % 4 == lane // 32) & (jnp.abs(slot - (r % 4).astype(F32)) < 0.5)
        one = jnp.where(here, member, 0.0)
        wsum = jnp.where(here, weight, 0.0)
        hi = wsum.astype(BF)
        lo = (wsum - hi.astype(F32)).astype(BF)
        m01[pl.ds(r0, 128), :] = one.astype(BF)
        mg[pl.ds(r0, 128), 0:128] = hi
        mg[pl.ds(r0, 128), 128:256] = lo
        one_t = jnp.transpose(one)
        w_t = jnp.transpose(wsum)
        hi_t = w_t.astype(BF)
        c01[:, pl.ds(r0, 128)] = one_t.astype(BF)
        cw[0:128, pl.ds(r0, 128)] = hi_t
        cw[128:256, pl.ds(r0, 128)] = (w_t - hi_t.astype(F32)).astype(BF)
        return carry

    lax.fori_loop(0, 8, place, 0)

    def scatter_units(src, dst, s_sem, r_sem, lo=1, hi=CHIPS):
        def one(i, carry):
            d2, t2 = peer(i)
            send(src.at[d2 * 8 + t2], dst.at[chip], s_sem, r_sem.at[chip // 16], (d2, t2 * 2 + c))
            return carry

        lax.fori_loop(lo, hi, one, 0)
        if hi == CHIPS:
            pltpu.make_async_copy(src.at[chip], dst.at[chip], r_sem.at[chip // 16]).start()

    def sent_units(src, s_sem):
        landed(src.at[pl.ds(0, CHIPS - 1)], s_sem)

    for q in range(4):
        for b in range(2):
            part = cot2[b, :, q * quarter : (q + 1) * quarter]
            row = q * 32 + b * 16
            cg[row : row + 16, :] = part
            cg[128 + row : 128 + row + 16, :] = part

    def place_cot(g, carry):
        rows = mm(mg[pl.ds(pl.multiple_of(g * 256, 256), 256), :], cg[...])
        buf_a[pl.ds(g * 16, 16)] = rows.astype(BF).reshape(16, ROWS, quarter)
        return carry

    lax.fori_loop(0, 4, place_cot, 0)
    scatter_units(buf_a, garr, ga_s, ga_r, 1, EARLY)

    for h in range(2):
        landed(block(h), dg_r.at[h])

    def turn(i):
        return (z + i + i // 2 - i // 3 * 2) % 4

    def dense(i, carry):
        m = turn(i)
        landed(hid.at[m], hg_r.at[m])
        pf[m] = mm_t(jnp.transpose(hid[m]), down_t[...]).reshape(16, 16, quarter)

        def pack(t, carry):
            psend[m, t] = pf[m, 2 * t + 1 - c].astype(BF)
            return carry

        lax.fori_loop(0, 8, pack, 0)
        send(psend.at[m], prec.at[m], ps_s.at[m], ps_r.at[m], partner)
        return carry

    lax.fori_loop(0, 4, dense, 0)

    def reduce(i, carry):
        m = turn(i)
        landed(prec.at[m], ps_r.at[m])

        def add(t, carry):
            rs_send[m, t] = (pf[m, 2 * t + c] + prec[m, t].astype(F32)).astype(BF)
            return carry

        lax.fori_loop(0, 8, add, 0)

        def out(k, carry):
            t2 = ((tc // 4 + k // 4) % 2) * 4 + (y + k % 4) % 4
            send(rs_send.at[m, t2], rs_recv.at[m, tc], rs_s.at[m], rs_r.at[m], (dp, t2 * 2 + c))
            return carry

        lax.fori_loop(1, 8, out, 0)
        pltpu.make_async_copy(rs_send.at[m, tc], rs_recv.at[m, tc], rs_r.at[m]).start()
        return carry

    lax.fori_loop(0, 4, reduce, 0)

    def sums_sent():
        def one(m, carry):
            landed(psend.at[m], ps_s.at[m])
            landed(rs_send.at[m, pl.ds(0, 7)], rs_s.at[m])
            return carry

        lax.fori_loop(0, 4, one, 0)

    pending.append(sums_sent)

    def to_owner(i, carry):
        m = turn(i)
        landed(rs_recv.at[m], rs_r.at[m])
        total = rs_recv[m, 0].astype(F32)
        for t in range(1, 8):
            total = total + rs_recv[m, t].astype(F32)
        zxs[m] = total

        @pl.when(i > 0)
        def _():
            send(zxs.at[m], zxr.at[z], zx_s.at[m], zx_r.at[z], (xh * 4 + m, tn))

        return carry

    lax.fori_loop(0, 4, to_owner, 0)
    scatter_units(buf_a, garr, ga_s, ga_r, EARLY, CHIPS)
    pltpu.make_async_copy(zxs.at[z], zxr.at[z], zx_r.at[z]).start()

    def owner_sent():
        for k in range(1, 4):
            landed(zxs.at[0], zx_s.at[(z + k) % 4])

    pending.append(owner_sent)
    for m in range(4):
        landed(zxr.at[m], zx_r.at[m])
        for h in range(2):
            at = (4 * h + m) * half
            dense_f[:, at : at + half] = zxr[m, :, h * half : (h + 1) * half]
    st = (res[...].astype(F32) + dense_f[...]).astype(BF)
    stream[...] = st
    st = st.astype(F32)
    square = jnp.sum(st * st, axis=1, keepdims=True)
    inverse = lax.rsqrt(square / width + 1e-6)
    nrm2[c] = (stream[...].astype(F32) * inverse * gain[...].astype(F32)).astype(BF)
    nx = send(nrm2.at[c], nrm2.at[c], ex_s.at[3], ex_r.at[3], partner)
    nx.wait_recv()
    pending.append(nx.wait_send)

    for q in range(4):
        for b in range(2):
            row = q * 32 + b * 16
            cn[row : row + 16, :] = nrm2[b, :, q * quarter : (q + 1) * quarter]

    def place_nrm(g, carry):
        rows = mm(m01[pl.ds(pl.multiple_of(g * 256, 256), 256), :], cn[...])
        buf_b[pl.ds(g * 16, 16)] = rows.astype(BF).reshape(16, ROWS, quarter)
        return carry

    lax.fori_loop(0, 4, place_nrm, 0)
    scatter_units(buf_b, narr, na_s, na_r)

    down2[...] = jnp.transpose(down_t[...])

    def collect(arr, r_sem):
        def group(g, carry):
            landed(arr.at[pl.ds(g * 16, 16)], r_sem.at[g])
            rows = mm(perm[...], arr[pl.ds(g * 16, 16)].reshape(256, quarter)).astype(BF)
            for q in range(4):
                xin[pl.ds(pl.multiple_of(g * 64, 64), 64), q * quarter : (q + 1) * quarter] = rows[
                    q * 64 : (q + 1) * 64
                ]
            return carry

        lax.fori_loop(0, 4, group, 0)

    collect(garr, ga_r)
    load_wd.wait()

    def back_down(n, carry):
        at = pl.ds(pl.multiple_of(n * 256, 256), 256)
        gact[:, at] = mm_t(xin[...], wd[at, :])
        return carry

    lax.fori_loop(0, 4, back_down, 0)

    collect(narr, na_r)
    load_wg.wait()
    load_wu.wait()

    def forward(n, carry):
        at = pl.ds(pl.multiple_of(n * 256, 256), 256)
        gate = mm(xin[...], wg[:, at])
        up = mm(xin[...], wu[:, at])
        ga = gact[:, at]
        s = jax.nn.sigmoid(gate)
        silu = gate * s
        act[:, at] = (silu * up).astype(BF)
        gg[:, at] = (ga * up * s * (1.0 + gate * (1.0 - s))).astype(BF)
        gu[:, at] = (ga * silu).astype(BF)
        return carry

    lax.fori_loop(0, 4, forward, 0)

    def to_zin(q, rows):
        rows = rows.astype(BF)
        for g in range(4):
            zin[g, pl.ds(pl.multiple_of(q * 64, 64), 64), :] = rows[g * 64 : (g + 1) * 64]

    def back_in(q, carry):
        at = pl.ds(pl.multiple_of(q * quarter, 128), quarter)
        to_zin(q, mm_t(gg[...], wg[at, :]) + mm_t(gu[...], wu[at, :]))
        return carry

    def from_zin(buf):
        def group(g, carry):
            rows = mm(perm_t[...], zin[g])
            buf[pl.ds(g * 16, 16)] = rows.astype(BF).reshape(16, ROWS, quarter)
            return carry

        lax.fori_loop(0, 4, group, 0)

    lax.fori_loop(0, 4, back_in, 0)
    sent_units(buf_b, na_s)
    from_zin(buf_b)
    scatter_units(buf_b, hret, ha_s, ha_r)
    pending.append(lambda: sent_units(buf_b, ha_s))

    def down_out(q, carry):
        at = pl.ds(pl.multiple_of(q * quarter, 128), quarter)
        to_zin(q, mm(act[...], wd[:, at]))
        return carry

    lax.fori_loop(0, 4, down_out, 0)
    sent_units(buf_a, ga_s)
    from_zin(buf_a)
    scatter_units(buf_a, eret, ea_s, ea_r)
    pending.append(lambda: sent_units(buf_a, ea_s))

    def share(u):
        def pack(q, carry):
            pax[u, q] = acc[u, 2 * q + 1 - c]
            return carry

        lax.fori_loop(0, 4, pack, 0)
        return send(pax.at[u], prx.at[u], px_s.at[u], px_r.at[u], partner)

    def summed(u, q):
        return acc[u, 2 * q + c] + prx[u, q]

    total = jnp.zeros((128, quarter), F32)
    for g in range(4):
        landed(hret.at[pl.ds(g * 16, 16)], ha_r.at[g])
        total = total + mm(c01[:, g * 256 : (g + 1) * 256], hret[g * 16 : (g + 1) * 16].reshape(256, quarter))
    acc[0] = total.reshape(8, 16, quarter)
    sh0 = share(0)
    sh0.wait_recv()
    pending.append(sh0.wait_send)

    dots = jnp.zeros((16, 1), F32)
    for q in range(4):
        cols = slice(q * quarter, (q + 1) * quarter)
        scaled = summed(0, q) * gain[:, cols].astype(F32)
        dots = dots + jnp.sum(scaled * (stream[:, cols].astype(F32) * inverse), axis=1, keepdims=True)
    mean = dots / width
    for q in range(4):
        cols = slice(q * quarter, (q + 1) * quarter)
        scaled = summed(0, q) * gain[:, cols].astype(F32)
        unit = stream[:, cols].astype(F32) * inverse
        gs_o[:, cols] = (cot[:, cols].astype(F32) + inverse * (scaled - unit * mean)).astype(BF)

    for m in range(4):
        for h in range(2):
            at = (4 * h + m) * half
            gsp[m, :, h * half : (h + 1) * half] = gs_o[:, at : at + half]
    for k in (2, 1, 3):
        to = (z + k) % 4
        pending.append(send(gsp.at[to], gs_all.at[tn, z], gx_s.at[k], gx_r.at[z], over_z[k]).wait_send)
    pltpu.make_async_copy(gsp.at[z], gs_all.at[tn, z], gx_r.at[z]).start()
    for m in range(4):
        landed(gs_all.at[tn, m], gx_r.at[m])

    def gather_gs(k, carry):
        t2 = ((tc // 4 + k // 4) % 2) * 4 + (y + k % 4) % 4
        send(gs_all.at[tn], gs_all.at[tn], gs_s.at[k], gs_r.at[tc], (dp, t2 * 2 + c))
        return carry

    lax.fori_loop(1, 8, gather_gs, 0)
    send(gs_all.at[tn], gs_all.at[tn], fw_s.at[tc], fw_r.at[tc], partner)

    def forward_gs(k, carry):
        t2 = ((tc // 4 + k // 4) % 2) * 4 + (y + k % 4) % 4
        b2 = t2 * 2 + c
        landed(gs_all.at[b2], gs_r.at[t2])
        send(gs_all.at[b2], gs_all.at[b2], fw_s.at[t2], fw_r.at[t2], partner)
        return carry

    lax.fori_loop(1, 8, forward_gs, 0)

    def gs_sent():
        def one(k, carry):
            landed(gs_all.at[0], gs_s.at[k])
            return carry

        lax.fori_loop(1, 8, one, 0)

        def two(k, carry):
            landed(gs_all.at[0], fw_s.at[k])
            return carry

        lax.fori_loop(0, 8, two, 0)

    pending.append(gs_sent)

    def all_gs(t, carry):
        landed(gs_all.at[t * 2 + 1 - c], fw_r.at[t])
        return carry

    lax.fori_loop(0, 8, all_gs, 0)
    for k in (2, 1, 3, 0):
        to = (z + k) % 4
        gh = mm_t(down2[...], gs_all[:, to].reshape(256, quarter))
        ghs[k] = gh.astype(BF)
        if k:
            pending.append(send(ghs.at[k], ghr.at[z], gh_s.at[k], gh_r.at[z], over_z[k]).wait_send)

    total = jnp.zeros((256, quarter), F32)
    for g in range(4):
        landed(eret.at[pl.ds(g * 16, 16)], ea_r.at[g])
        total = total + mm(cw[:, g * 256 : (g + 1) * 256], eret[g * 16 : (g + 1) * 16].reshape(256, quarter))
    acc[1] = (total[0:128] + total[128:256]).reshape(8, 16, quarter)
    sh1 = share(1)
    sh1.wait_recv()
    pending.append(sh1.wait_send)
    for q in range(4):
        cols = slice(q * quarter, (q + 1) * quarter)
        moe_o[:, cols] = (stream[:, cols].astype(F32) + summed(1, q)).astype(BF)

    for k in (1, 3, 2):
        at = (z + k) % 4
        landed(ghr.at[at], gh_r.at[at])
        gh = gh + ghr[at].astype(F32)
    gh_o[...] = gh.astype(BF)

    drain()


def hand_over(a, b, c, a_o, b_o, c_o):
    a_o[...] = a[...]
    b_o[...] = b[...]
    c_o[...] = c[...]


def body(
    dense_hidden, dense_down, residual, norm_gain, expert_ids, route_weights,
    w_gate, w_up, w_down, out_cotangent,
):
    width = residual.shape[1]
    q = width // 4
    hidden_units, cols = dense_down.shape
    fe = w_gate.shape[2]

    vmem = pl.BlockSpec(memory_space=pltpu.VMEM)
    hbm = pl.BlockSpec(memory_space=pl.ANY)
    V = pltpu.VMEM
    dma = pltpu.SemaphoreType.DMA
    unit = (CHIPS, ROWS, q)
    scratch = [
        V((4, hidden_units, 256), BF), V((2 * cols, hidden_units), BF), V((hidden_units, q), BF),
        V((width, fe), BF), V((width, fe), BF), V((fe, width), BF),
        V((1, width), BF), V((2, 16, width), BF), V((2, 8, 128), F32), V((2, 8, 128), F32), V((2, 16, width), BF),
        V((1024, 128), BF), V((1024, 256), BF), V((128, 1024), BF), V((256, 1024), BF),
        V((256, 256), BF), V((256, 256), BF), V((128, q), BF), V((256, q), BF),
        V(unit, BF), V(unit, BF), V(unit, BF), V(unit, BF), V(unit, BF), V(unit, BF),
        V((256, width), BF), V((256, fe), F32), V((256, fe), BF), V((256, fe), BF), V((256, fe), BF),
        V((4, 256, q), BF),
        V((4, 16, 16, q), F32), V((4, 8, 16, q), BF), V((4, 8, 16, q), BF), V((4, 8, 16, q), BF),
        V((4, 8, 16, q), BF), V((4, 16, q), F32), V((4, 16, q), F32), V((16, width), F32), V((16, width), BF),
        V((2, 8, 16, q), F32), V((2, 4, 16, q), F32), V((2, 4, 16, q), F32), V((4, 16, q), BF), V((16, 4, 16, q), BF),
        V((4, hidden_units, 256), BF), V((4, hidden_units, 256), BF),
        dma((4,)), dma((4,)), dma((4,)), dma((4,)), dma((4,)), dma, dma((2,)), dma((4,)), dma((4,)), dma((4,)), dma((4,)), dma((4,)), dma((4,)), dma((4,)), dma((4,)), dma((4,)), dma((4,)),
        dma, dma((4,)), dma, dma((4,)), dma, dma((4,)), dma, dma((4,)),
        dma((2,)), dma((2,)), dma((8,)), dma((8,)), dma((8,)), dma((8,)),
    ]
    moe, gs, gh = pl.pallas_call(
        kernel,
        out_shape=(
            jax.ShapeDtypeStruct(residual.shape, BF),
            jax.ShapeDtypeStruct(residual.shape, BF),
            jax.ShapeDtypeStruct(dense_hidden.shape[::-1], BF),
        ),
        in_specs=[hbm, hbm, vmem, vmem, vmem, vmem, vmem, hbm, hbm, hbm],
        out_specs=(vmem, vmem, vmem),
        scratch_shapes=scratch,
        compiler_params=pltpu.CompilerParams(
            collective_id=0, has_side_effects=True, vmem_limit_bytes=63 * 1024 * 1024
        ),
    )(
        dense_hidden.T, dense_down.T, residual, norm_gain, out_cotangent, expert_ids.T, route_weights.T,
        w_gate[0], w_up[0], w_down[0],
    )
    moe, gs, gh = pl.pallas_call(
        hand_over,
        out_shape=tuple(jax.ShapeDtypeStruct(a.shape, a.dtype) for a in (moe, gs, gh)),
        in_specs=[vmem] * 3,
        out_specs=(vmem,) * 3,
    )(moe, gs, gh)
    return moe, gs, gh.T


def solution(mesh):
    rows = P(("dp", "tensor"), None)
    experts = P(("dp", "tensor"), None, None)
    placed = (P("dp", "tensor"), P("tensor", "dp"), rows, P(), rows, rows, experts, experts, experts, rows)
    return jax.shard_map(
        body, mesh=mesh, in_specs=placed, out_specs=(rows, rows, P("dp", "tensor")), check_vma=False
    )
```

```python
import jax
import jax.numpy as jnp
from jax import lax
from jax.experimental import pallas as pl
from jax.experimental.pallas import tpu as pltpu
from jax.sharding import PartitionSpec as P

MESH = pl.DeviceIdType.MESH
BF = jnp.bfloat16
F32 = jnp.float32
CHIPS = 64
COT = (6, 16)
OUT = (22, 14, 10, 2)
ROWS = 16
NT = (((1,), (1,)), ((), ()))


def mm(a, b):
    return jnp.dot(a, b, preferred_element_type=F32)


def mm_t(a, b):
    return lax.dot_general(a, b, NT, preferred_element_type=F32)


def landed(ref, sem):
    pltpu.make_async_copy(ref, ref, sem).wait()


def kernel(
    hid_h, down_h, res, gain_in, cot, ids_in, wt_in, wg_h, wu_h, wd_h,
    moe_o, gs_o, gh_o,
    hid, down_t, down2, wg, wu, wd,
    gain, cot2, key2, wt2, nrm2,
    m01, mg, c01, cw, perm, perm_t, cn, cg,
    buf_a, garr, buf_b, narr, hret, eret,
    xin, gates, ups, act, gg, gu, zin,
    pf, psend, prec, rs_send, rs_recv, zxs, zxr, dense_f, stream,
    acc, pax, prx, gsp, gs_all, ghs, ghr,
    loc, ex_s, ex_r, hg_s, hg_r, dg_s, dg_r, zx_s, zx_r, gx_s, gx_r, gh_s, gh_r, ps_s, ps_r, rs_s, rs_r,
    ga_s, ga_r, na_s, na_r, ha_s, ha_r, ea_s, ea_r, px_s, px_r, gs_s, gs_r, fw_s, fw_r,
):
    width = res.shape[1]
    quarter = width // 4
    half = quarter // 2
    dp = lax.axis_index("dp")
    tn = lax.axis_index("tensor")
    c = tn % 2
    tc = tn // 2
    chip = dp * 8 + tc
    z, y = dp % 4, tc % 4
    xh = dp // 4
    x = xh * 2 + tc // 4
    over_x = ((1 - xh) * 4 + z, tn)
    partner = (dp, tc * 2 + 1 - c)

    def peer(i):
        u = i // 4 % 4
        x2 = (x + i) % 4
        y2 = (y + i + u) % 4
        z2 = (z + i + 2 * u + i // 16) % 4
        return (x2 // 2) * 4 + z2, (x2 % 2) * 4 + y2

    def send(src, dst, s_sem, r_sem, device):
        copy = pltpu.make_async_remote_copy(
            src_ref=src, dst_ref=dst, send_sem=s_sem, recv_sem=r_sem,
            device_id=device, device_id_type=MESH,
        )
        copy.start()
        return copy

    pending = []

    def drain():
        for done in pending:
            done()

    def block(h):
        return down_t.at[pl.ds(pl.multiple_of(h * half, 16), half)]

    pltpu.make_async_copy(down_h, block(xh), dg_r.at[xh]).start()
    pltpu.make_async_copy(hid_h, hid.at[z], hg_r.at[z]).start()
    load_wd = pltpu.make_async_copy(wd_h, wd, loc.at[1])
    load_wg = pltpu.make_async_copy(wg_h, wg, loc.at[2])
    load_wu = pltpu.make_async_copy(wu_h, wu, loc.at[3])

    barrier = pltpu.get_barrier_semaphore()

    def greet(i, carry):
        d2, t2 = peer(i)
        pl.semaphore_signal(barrier, inc=1, device_id=(d2, t2 * 2 + c), device_id_type=MESH)
        return carry

    lax.fori_loop(1, CHIPS, greet, 0)
    pl.semaphore_signal(barrier, inc=1, device_id=partner, device_id_type=MESH)

    lane = lax.broadcasted_iota(jnp.int32, (16, 128), 1)
    spread = jnp.where(lane % 16 == lax.broadcasted_iota(jnp.int32, (16, 128), 0), 1.0, 0.0)

    def lanes(a):
        return jnp.dot(a, spread, precision=lax.Precision.HIGHEST, preferred_element_type=F32)

    key2[c] = lanes(ids_in[...].astype(F32))
    wt2[c] = lanes(wt_in[...])
    cot2[c] = cot[...]
    gain[...] = gain_in[...].reshape(1, width)
    pl.semaphore_wait(barrier, CHIPS)

    ex = [
        send(key2.at[c], key2.at[c], ex_s.at[1], ex_r.at[1], partner),
        send(wt2.at[c], wt2.at[c], ex_s.at[2], ex_r.at[2], partner),
        send(cot2.at[c], cot2.at[c], ex_s.at[0], ex_r.at[0], partner),
    ]

    over_z = [(xh * 4 + (z + k) % 4, tn) for k in range(4)]
    pending.append(send(down_h, block(xh), dg_s, dg_r.at[xh], over_x).wait_send)
    for k in (1, 3, 2):
        pending.append(send(hid_h, hid.at[z], hg_s.at[k], hg_r.at[z], over_z[k]).wait_send)

    load_wg.start()
    load_wu.start()
    load_wd.start()

    o = lax.broadcasted_iota(jnp.int32, (256, 256), 0)
    i = lax.broadcasted_iota(jnp.int32, (256, 256), 1)
    perm[...] = jnp.where((o % 64) // 4 * 16 + o // 64 * 4 + o % 4 == i, 1.0, 0.0).astype(BF)
    perm_t[...] = jnp.where((i % 64) // 4 * 16 + i // 64 * 4 + i % 4 == o, 1.0, 0.0).astype(BF)

    pending.extend(e.wait_send for e in ex)
    for e in ex:
        e.wait_recv()

    row = lax.broadcasted_iota(jnp.int32, (128, 128), 0)
    lane = lax.broadcasted_iota(jnp.int32, (128, 128), 1)
    earlier = jnp.where((row // 16 == lane // 16) & (row < lane), 1.0, 0.0).astype(BF)
    first = (lax.broadcasted_iota(jnp.int32, (8, 128), 1) // 16) % 2 == 0
    keys = jnp.where(first, key2[0], key2[1])
    wts = jnp.where(first, wt2[0], wt2[1])

    def place(n, carry):
        r0 = pl.multiple_of(n * 128, 128)
        r = r0 + row
        expert = ((r // 16) * 2 + c).astype(F32)
        member = jnp.zeros((128, 128), F32)
        weight = jnp.zeros((128, 128), F32)
        for k in range(8):
            hit = jnp.abs(keys[k : k + 1, :] - expert) < 0.5
            member = jnp.where(hit, 1.0, member)
            weight = jnp.where(hit, wts[k : k + 1, :], weight)
        slot = mm(member.astype(BF), earlier) + (lane // 16 % 2 * 2).astype(F32)
        here = ((r // 4) % 4 == lane // 32) & (jnp.abs(slot - (r % 4).astype(F32)) < 0.5)
        one = jnp.where(here, member, 0.0)
        wsum = jnp.where(here, weight, 0.0)
        hi = wsum.astype(BF)
        lo = (wsum - hi.astype(F32)).astype(BF)
        m01[pl.ds(r0, 128), :] = one.astype(BF)
        mg[pl.ds(r0, 128), 0:128] = hi
        mg[pl.ds(r0, 128), 128:256] = lo
        one_t = jnp.transpose(one)
        w_t = jnp.transpose(wsum)
        hi_t = w_t.astype(BF)
        c01[:, pl.ds(r0, 128)] = one_t.astype(BF)
        cw[0:128, pl.ds(r0, 128)] = hi_t
        cw[128:256, pl.ds(r0, 128)] = (w_t - hi_t.astype(F32)).astype(BF)
        return carry

    lax.fori_loop(0, 8, place, 0)

    def some_units(src, dst, s_sem, r_sem, lo, count):
        def one(i, carry):
            d2, t2 = peer(lo + i)
            send(src.at[d2 * 8 + t2], dst.at[chip], s_sem, r_sem.at[chip // 16], (d2, t2 * 2 + c))
            return carry

        lax.fori_loop(0, count, one, 0)

    def scatter_units(src, dst, s_sem, r_sem, lo=1):
        some_units(src, dst, s_sem, r_sem, lo, CHIPS - lo)
        pltpu.make_async_copy(src.at[chip], dst.at[chip], r_sem.at[chip // 16]).start()

    def sent_units(src, s_sem):
        landed(src.at[pl.ds(0, CHIPS - 1)], s_sem)

    for q in range(4):
        for b in range(2):
            part = cot2[b, :, q * quarter : (q + 1) * quarter]
            row = q * 32 + b * 16
            cg[row : row + 16, :] = part
            cg[128 + row : 128 + row + 16, :] = part

    def place_cot(g, carry):
        rows = mm(mg[pl.ds(pl.multiple_of(g * 256, 256), 256), :], cg[...])
        buf_a[pl.ds(g * 16, 16)] = rows.astype(BF).reshape(16, ROWS, quarter)
        return carry

    lax.fori_loop(0, 4, place_cot, 0)

    def cot_units(lo, count):
        some_units(buf_a, garr, ga_s, ga_r, lo, count)

    cot_units(1, COT[0])
    next_cot = 1 + COT[0]

    for h in range(2):
        landed(block(h), dg_r.at[h])

    def turn(i):
        return (z + i + i // 2 - i // 3 * 2) % 4

    def dense(i, carry):
        m = turn(i)
        landed(hid.at[m], hg_r.at[m])
        pf[m] = mm_t(jnp.transpose(hid[m]), down_t[...]).reshape(16, 16, quarter)

        def pack(t, carry):
            psend[m, t] = pf[m, 2 * t + 1 - c].astype(BF)
            return carry

        lax.fori_loop(0, 8, pack, 0)
        send(psend.at[m], prec.at[m], ps_s.at[m], ps_r.at[m], partner)
        return carry

    lax.fori_loop(0, 4, dense, 0)

    def reduce(i, carry):
        m = turn(i)
        landed(prec.at[m], ps_r.at[m])

        def add(t, carry):
            rs_send[m, t] = (pf[m, 2 * t + c] + prec[m, t].astype(F32)).astype(BF)
            return carry

        lax.fori_loop(0, 8, add, 0)

        def out(k, carry):
            t2 = ((tc // 4 + k // 4) % 2) * 4 + (y + k % 4) % 4
            send(rs_send.at[m, t2], rs_recv.at[m, tc], rs_s.at[m], rs_r.at[m], (dp, t2 * 2 + c))
            return carry

        lax.fori_loop(1, 8, out, 0)
        pltpu.make_async_copy(rs_send.at[m, tc], rs_recv.at[m, tc], rs_r.at[m]).start()
        return carry

    lax.fori_loop(0, 4, reduce, 0)

    def sums_sent():
        def one(m, carry):
            landed(psend.at[m], ps_s.at[m])
            landed(rs_send.at[m, pl.ds(0, 7)], rs_s.at[m])
            return carry

        lax.fori_loop(0, 4, one, 0)

    pending.append(sums_sent)

    def to_owner(i, carry):
        m = turn(i)
        landed(rs_recv.at[m], rs_r.at[m])
        total = rs_recv[m, 0].astype(F32)
        for t in range(1, 8):
            total = total + rs_recv[m, t].astype(F32)
        zxs[m] = total

        @pl.when(i > 0)
        def _():
            send(zxs.at[m], zxr.at[z], zx_s.at[m], zx_r.at[z], (xh * 4 + m, tn))

        return carry

    lax.fori_loop(0, 4, to_owner, 0)
    cot_units(next_cot, COT[1])
    next_cot = next_cot + COT[1]
    pltpu.make_async_copy(zxs.at[z], zxr.at[z], zx_r.at[z]).start()

    def owner_sent():
        for k in range(1, 4):
            landed(zxs.at[0], zx_s.at[(z + k) % 4])

    pending.append(owner_sent)
    for m in range(4):
        landed(zxr.at[m], zx_r.at[m])
        for h in range(2):
            at = (4 * h + m) * half
            dense_f[:, at : at + half] = zxr[m, :, h * half : (h + 1) * half]
    st = (res[...].astype(F32) + dense_f[...]).astype(BF)
    stream[...] = st
    st = st.astype(F32)
    square = jnp.sum(st * st, axis=1, keepdims=True)
    inverse = lax.rsqrt(square / width + 1e-6)
    nrm2[c] = (stream[...].astype(F32) * inverse * gain[...].astype(F32)).astype(BF)
    nx = send(nrm2.at[c], nrm2.at[c], ex_s.at[3], ex_r.at[3], partner)
    nx.wait_recv()
    pending.append(nx.wait_send)

    for q in range(4):
        for b in range(2):
            row = q * 32 + b * 16
            cn[row : row + 16, :] = nrm2[b, :, q * quarter : (q + 1) * quarter]

    def place_nrm(g, carry):
        rows = mm(m01[pl.ds(pl.multiple_of(g * 256, 256), 256), :], cn[...])
        buf_b[pl.ds(g * 16, 16)] = rows.astype(BF).reshape(16, ROWS, quarter)
        return carry

    lax.fori_loop(0, 4, place_nrm, 0)
    scatter_units(buf_b, narr, na_s, na_r)
    scatter_units(buf_a, garr, ga_s, ga_r, next_cot)

    down2[...] = jnp.transpose(down_t[...])

    def collect(arr, r_sem):
        def group(g, carry):
            landed(arr.at[pl.ds(g * 16, 16)], r_sem.at[g])
            rows = mm(perm[...], arr[pl.ds(g * 16, 16)].reshape(256, quarter)).astype(BF)
            for q in range(4):
                xin[pl.ds(pl.multiple_of(g * 64, 64), 64), q * quarter : (q + 1) * quarter] = rows[
                    q * 64 : (q + 1) * 64
                ]
            return carry

        lax.fori_loop(0, 4, group, 0)

    collect(narr, na_r)
    load_wd.wait()
    load_wg.wait()
    load_wu.wait()

    def forward(n, carry):
        at = pl.ds(pl.multiple_of(n * 256, 256), 256)
        gate = mm(xin[...], wg[:, at])
        up = mm(xin[...], wu[:, at])
        gates[:, at] = gate
        ups[:, at] = up
        act[:, at] = (gate * jax.nn.sigmoid(gate) * up).astype(BF)
        return carry

    lax.fori_loop(0, 4, forward, 0)

    def backward(n, carry):
        at = pl.ds(pl.multiple_of(n * 256, 256), 256)
        ga = mm_t(xin[...], wd[at, :])
        gate = gates[:, at]
        s = jax.nn.sigmoid(gate)
        gg[:, at] = (ga * ups[:, at] * s * (1.0 + gate * (1.0 - s))).astype(BF)
        gu[:, at] = (ga * (gate * s)).astype(BF)
        return carry

    def to_zin(q, rows):
        rows = rows.astype(BF)
        for g in range(4):
            zin[g, pl.ds(pl.multiple_of(q * 64, 64), 64), :] = rows[g * 64 : (g + 1) * 64]

    def back_in(q, carry):
        at = pl.ds(pl.multiple_of(q * quarter, 128), quarter)
        to_zin(q, mm_t(gg[...], wg[at, :]) + mm_t(gu[...], wu[at, :]))
        return carry

    def from_zin(buf):
        def group(g, carry):
            rows = mm(perm_t[...], zin[g])
            buf[pl.ds(g * 16, 16)] = rows.astype(BF).reshape(16, ROWS, quarter)
            return carry

        lax.fori_loop(0, 4, group, 0)

    def down_out(q, carry):
        at = pl.ds(pl.multiple_of(q * quarter, 128), quarter)
        to_zin(q, mm(act[...], wd[:, at]))
        return carry

    def out_units(lo, count):
        some_units(buf_b, eret, ea_s, ea_r, lo, count)

    lax.fori_loop(0, 4, down_out, 0)
    sent_units(buf_b, na_s)
    from_zin(buf_b)
    out_units(1, OUT[0])
    collect(garr, ga_r)
    lax.fori_loop(0, 4, backward, 0)
    lax.fori_loop(0, 4, back_in, 0)
    sent_units(buf_a, ga_s)
    from_zin(buf_a)
    scatter_units(buf_a, hret, ha_s, ha_r)
    pending.append(lambda: sent_units(buf_a, ha_s))
    out_units(1 + OUT[0], OUT[1])
    next_out = 1 + OUT[0] + OUT[1]

    def share(u):
        def pack(q, carry):
            pax[u, q] = acc[u, 2 * q + 1 - c]
            return carry

        lax.fori_loop(0, 4, pack, 0)
        return send(pax.at[u], prx.at[u], px_s.at[u], px_r.at[u], partner)

    def summed(u, q):
        return acc[u, 2 * q + c] + prx[u, q]

    total = jnp.zeros((128, quarter), F32)
    for g in range(4):
        landed(hret.at[pl.ds(g * 16, 16)], ha_r.at[g])
        total = total + mm(c01[:, g * 256 : (g + 1) * 256], hret[g * 16 : (g + 1) * 16].reshape(256, quarter))
    acc[0] = total.reshape(8, 16, quarter)
    sh0 = share(0)
    sh0.wait_recv()
    pending.append(sh0.wait_send)

    dots = jnp.zeros((16, 1), F32)
    for q in range(4):
        cols = slice(q * quarter, (q + 1) * quarter)
        scaled = summed(0, q) * gain[:, cols].astype(F32)
        dots = dots + jnp.sum(scaled * (stream[:, cols].astype(F32) * inverse), axis=1, keepdims=True)
    mean = dots / width
    for q in range(4):
        cols = slice(q * quarter, (q + 1) * quarter)
        scaled = summed(0, q) * gain[:, cols].astype(F32)
        unit = stream[:, cols].astype(F32) * inverse
        gs_o[:, cols] = (cot[:, cols].astype(F32) + inverse * (scaled - unit * mean)).astype(BF)

    for m in range(4):
        for h in range(2):
            at = (4 * h + m) * half
            gsp[m, :, h * half : (h + 1) * half] = gs_o[:, at : at + half]
    for k in (2, 1, 3):
        to = (z + k) % 4
        pending.append(send(gsp.at[to], gs_all.at[tn, z], gx_s.at[k], gx_r.at[z], over_z[k]).wait_send)
    pltpu.make_async_copy(gsp.at[z], gs_all.at[tn, z], gx_r.at[z]).start()
    out_units(next_out, OUT[2])
    next_out2 = next_out + OUT[2]
    next_out2 = next_out + OUT[2]
    for n, k in enumerate((1, 3, 2, 0)):
        m = (z + k) % 4
        landed(gs_all.at[tn, m], gx_r.at[m])

        def gather_gs(i, carry):
            t2 = ((tc // 4 + i // 4) % 2) * 4 + (y + i % 4) % 4
            send(gs_all.at[tn, m], gs_all.at[tn, m], gs_s.at[m], gs_r.at[m, tc], (dp, t2 * 2 + c))
            return carry

        lax.fori_loop(1, 8, gather_gs, 0)
        send(gs_all.at[tn, m], gs_all.at[tn, m], fw_s.at[m], fw_r.at[m, tc], partner)
        out_units(next_out2 + n * OUT[3], OUT[3])

    for k in (1, 3, 2, 0):
        m = (z + k) % 4

        def forward_gs(i, carry):
            t2 = ((tc // 4 + i // 4) % 2) * 4 + (y + i % 4) % 4
            b2 = t2 * 2 + c
            landed(gs_all.at[b2, m], gs_r.at[m, t2])
            send(gs_all.at[b2, m], gs_all.at[b2, m], fw_s.at[m], fw_r.at[m, t2], partner)
            return carry

        lax.fori_loop(1, 8, forward_gs, 0)

        def all_gs(t, carry):
            landed(gs_all.at[t * 2 + 1 - c, m], fw_r.at[m, t])
            return carry

        lax.fori_loop(0, 8, all_gs, 0)
        gh = mm_t(down2[...], gs_all[:, m].reshape(256, quarter))
        if k:
            ghs[k] = gh.astype(BF)
            pending.append(send(ghs.at[k], ghr.at[z], gh_s.at[k], gh_r.at[z], over_z[k]).wait_send)

    def gs_sent():
        for m in range(4):
            landed(gs_all.at[pl.ds(0, 7), 0], gs_s.at[m])
            landed(gs_all.at[pl.ds(0, 8), 0], fw_s.at[m])

    pending.append(gs_sent)
    scatter_units(buf_b, eret, ea_s, ea_r, next_out2 + 4 * OUT[3])
    pending.append(lambda: sent_units(buf_b, ea_s))

    total = jnp.zeros((256, quarter), F32)
    for g in range(4):
        landed(eret.at[pl.ds(g * 16, 16)], ea_r.at[g])
        total = total + mm(cw[:, g * 256 : (g + 1) * 256], eret[g * 16 : (g + 1) * 16].reshape(256, quarter))
    acc[1] = (total[0:128] + total[128:256]).reshape(8, 16, quarter)
    sh1 = share(1)
    sh1.wait_recv()
    pending.append(sh1.wait_send)
    for q in range(4):
        cols = slice(q * quarter, (q + 1) * quarter)
        moe_o[:, cols] = (stream[:, cols].astype(F32) + summed(1, q)).astype(BF)

    for k in (1, 3, 2):
        at = (z + k) % 4
        landed(ghr.at[at], gh_r.at[at])
        gh = gh + ghr[at].astype(F32)
    gh_o[...] = gh.astype(BF)

    drain()


def hand_over(a, b, c, a_o, b_o, c_o):
    a_o[...] = a[...]
    b_o[...] = b[...]
    c_o[...] = c[...]


def body(
    dense_hidden, dense_down, residual, norm_gain, expert_ids, route_weights,
    w_gate, w_up, w_down, out_cotangent,
):
    width = residual.shape[1]
    q = width // 4
    hidden_units, cols = dense_down.shape
    fe = w_gate.shape[2]

    vmem = pl.BlockSpec(memory_space=pltpu.VMEM)
    hbm = pl.BlockSpec(memory_space=pl.ANY)
    V = pltpu.VMEM
    dma = pltpu.SemaphoreType.DMA
    unit = (CHIPS, ROWS, q)
    scratch = [
        V((4, hidden_units, 256), BF), V((2 * cols, hidden_units), BF), V((hidden_units, q), BF),
        V((width, fe), BF), V((width, fe), BF), V((fe, width), BF),
        V((1, width), BF), V((2, 16, width), BF), V((2, 8, 128), F32), V((2, 8, 128), F32), V((2, 16, width), BF),
        V((1024, 128), BF), V((1024, 256), BF), V((128, 1024), BF), V((256, 1024), BF),
        V((256, 256), BF), V((256, 256), BF), V((128, q), BF), V((256, q), BF),
        V(unit, BF), V(unit, BF), V(unit, BF), V(unit, BF), V(unit, BF), V(unit, BF),
        V((256, width), BF), V((256, fe), F32), V((256, fe), F32), V((256, fe), BF), V((256, fe), BF), V((256, fe), BF),
        V((4, 256, q), BF),
        V((4, 16, 16, q), F32), V((4, 8, 16, q), BF), V((4, 8, 16, q), BF), V((4, 8, 16, q), BF),
        V((4, 8, 16, q), BF), V((4, 16, q), F32), V((4, 16, q), F32), V((16, width), F32), V((16, width), BF),
        V((2, 8, 16, q), F32), V((2, 4, 16, q), F32), V((2, 4, 16, q), F32), V((4, 16, q), BF), V((16, 4, 16, q), BF),
        V((4, hidden_units, 256), BF), V((4, hidden_units, 256), BF),
        dma((4,)), dma((4,)), dma((4,)), dma((4,)), dma((4,)), dma, dma((2,)), dma((4,)), dma((4,)), dma((4,)), dma((4,)), dma((4,)), dma((4,)), dma((4,)), dma((4,)), dma((4,)), dma((4,)),
        dma, dma((4,)), dma, dma((4,)), dma, dma((4,)), dma, dma((4,)),
        dma((2,)), dma((2,)), dma((4,)), dma((4, 8)), dma((4,)), dma((4, 8)),
    ]
    moe, gs, gh = pl.pallas_call(
        kernel,
        out_shape=(
            jax.ShapeDtypeStruct(residual.shape, BF),
            jax.ShapeDtypeStruct(residual.shape, BF),
            jax.ShapeDtypeStruct(dense_hidden.shape[::-1], BF),
        ),
        in_specs=[hbm, hbm, vmem, vmem, vmem, vmem, vmem, hbm, hbm, hbm],
        out_specs=(vmem, vmem, vmem),
        scratch_shapes=scratch,
        compiler_params=pltpu.CompilerParams(
            collective_id=0, has_side_effects=True, vmem_limit_bytes=63 * 1024 * 1024
        ),
    )(
        dense_hidden.T, dense_down.T, residual, norm_gain, out_cotangent, expert_ids.T, route_weights.T,
        w_gate[0], w_up[0], w_down[0],
    )
    moe, gs, gh = pl.pallas_call(
        hand_over,
        out_shape=tuple(jax.ShapeDtypeStruct(a.shape, a.dtype) for a in (moe, gs, gh)),
        in_specs=[vmem] * 3,
        out_specs=(vmem,) * 3,
    )(moe, gs, gh)
    return moe, gs, gh.T


def solution(mesh):
    rows = P(("dp", "tensor"), None)
    experts = P(("dp", "tensor"), None, None)
    placed = (P("dp", "tensor"), P("tensor", "dp"), rows, P(), rows, rows, experts, experts, experts, rows)
    return jax.shard_map(
        body, mesh=mesh, in_specs=placed, out_specs=(rows, rows, P("dp", "tensor")), check_vma=False
    )
```

```python
import jax
import jax.numpy as jnp
from jax import lax
from jax.experimental import pallas as pl
from jax.experimental.pallas import tpu as pltpu
from jax.sharding import PartitionSpec as P

MESH = pl.DeviceIdType.MESH
BF = jnp.bfloat16
F32 = jnp.float32
CHIPS = 64
COT = (0, 26)
OUT = (28, 20, 8, 1)
ROWS = 16
NT = (((1,), (1,)), ((), ()))


def mm(a, b):
    return jnp.dot(a, b, preferred_element_type=F32)


def mm_t(a, b):
    return lax.dot_general(a, b, NT, preferred_element_type=F32)


def landed(ref, sem):
    pltpu.make_async_copy(ref, ref, sem).wait()


def kernel(
    hid_h, down_h, res, gain_in, cot, ids_in, wt_in, wg_h, wu_h, wd_h,
    moe_o, gs_o, gh_o,
    hid, down_t, down2, wg, wu, wd,
    gain, cot2, key2, wt2, nrm2,
    m01, mg, c01, cw, perm, perm_t, cn, cg,
    buf_a, garr, buf_b, narr, hret, eret,
    xin, gates, ups, act, gg, gu, zin,
    pf, psend, prec, rs_send, rs_recv, zxs, zxr, dense_f, stream,
    acc, pax, prx, gsp, gs_all, ghs, ghr,
    plane, space, loc, ex_s, ex_r, hg_s, hg_r, dg_s, dg_r, zx_s, zx_r, gx_s, gx_r, gh_s, gh_r, ps_s, ps_r, rs_s, rs_r,
    ga_s, ga_r, na_s, na_r, ha_s, ha_r, ea_s, ea_r, px_s, px_r, gs_s, gs_r, fw_s, fw_r,
):
    width = res.shape[1]
    quarter = width // 4
    half = quarter // 2
    dp = lax.axis_index("dp")
    tn = lax.axis_index("tensor")
    c = tn % 2
    tc = tn // 2
    chip = dp * 8 + tc
    z, y = dp % 4, tc % 4
    xh = dp // 4
    x = xh * 2 + tc // 4
    over_x = ((1 - xh) * 4 + z, tn)
    partner = (dp, tc * 2 + 1 - c)

    def peer(i):
        u = i // 4 % 4
        x2 = (x + i) % 4
        y2 = (y + i + u) % 4
        z2 = (z + i + 2 * u + i // 16) % 4
        return (x2 // 2) * 4 + z2, (x2 % 2) * 4 + y2

    def send(src, dst, s_sem, r_sem, device):
        copy = pltpu.make_async_remote_copy(
            src_ref=src, dst_ref=dst, send_sem=s_sem, recv_sem=r_sem,
            device_id=device, device_id_type=MESH,
        )
        copy.start()
        return copy

    pending = []

    def drain():
        for done in pending:
            done()

    def block(h):
        return down_t.at[pl.ds(pl.multiple_of(h * half, 16), half)]

    pltpu.make_async_copy(down_h, block(xh), dg_r.at[xh]).start()
    pltpu.make_async_copy(hid_h, hid.at[z], hg_r.at[z]).start()
    load_wd = pltpu.make_async_copy(wd_h, wd, loc.at[1])
    load_wg = pltpu.make_async_copy(wg_h, wg, loc.at[2])
    load_wu = pltpu.make_async_copy(wu_h, wu, loc.at[3])

    barrier = pltpu.get_barrier_semaphore()

    def on_line(dx, dy, dz):
        x2, y2, z2 = (x + dx) % 4, (y + dy) % 4, (z + dz) % 4
        return (x2 // 2) * 4 + z2, ((x2 % 2) * 4 + y2) * 2 + c

    def signal(sem, to):
        pl.semaphore_signal(sem, inc=1, device_id=to, device_id_type=MESH)

    signal(barrier, partner)
    for k in (1, 2, 3):
        signal(barrier, on_line(0, 0, k))
        signal(barrier, on_line(k, 0, 0))
        signal(barrier, on_line(0, k, 0))

    lane = lax.broadcasted_iota(jnp.int32, (16, 128), 1)
    spread = jnp.where(lane % 16 == lax.broadcasted_iota(jnp.int32, (16, 128), 0), 1.0, 0.0)

    def lanes(a):
        return jnp.dot(a, spread, precision=lax.Precision.HIGHEST, preferred_element_type=F32)

    key2[c] = lanes(ids_in[...].astype(F32))
    wt2[c] = lanes(wt_in[...])
    cot2[c] = cot[...]
    gain[...] = gain_in[...].reshape(1, width)
    pl.semaphore_wait(barrier, 10)
    for k in (1, 2, 3):
        signal(plane, on_line(0, k, 0))

    ex = [
        send(key2.at[c], key2.at[c], ex_s.at[1], ex_r.at[1], partner),
        send(wt2.at[c], wt2.at[c], ex_s.at[2], ex_r.at[2], partner),
        send(cot2.at[c], cot2.at[c], ex_s.at[0], ex_r.at[0], partner),
    ]

    over_z = [(xh * 4 + (z + k) % 4, tn) for k in range(4)]
    pending.append(send(down_h, block(xh), dg_s, dg_r.at[xh], over_x).wait_send)
    for k in (1, 3, 2):
        pending.append(send(hid_h, hid.at[z], hg_s.at[k], hg_r.at[z], over_z[k]).wait_send)

    load_wg.start()
    load_wu.start()
    load_wd.start()

    pl.semaphore_wait(plane, 3)
    for k in (1, 2, 3):
        signal(space, on_line(0, 0, k))

    o = lax.broadcasted_iota(jnp.int32, (256, 256), 0)
    i = lax.broadcasted_iota(jnp.int32, (256, 256), 1)
    perm[...] = jnp.where((o % 64) // 4 * 16 + o // 64 * 4 + o % 4 == i, 1.0, 0.0).astype(BF)
    perm_t[...] = jnp.where((i % 64) // 4 * 16 + i // 64 * 4 + i % 4 == o, 1.0, 0.0).astype(BF)

    pending.extend(e.wait_send for e in ex)
    for e in ex:
        e.wait_recv()

    row = lax.broadcasted_iota(jnp.int32, (128, 128), 0)
    lane = lax.broadcasted_iota(jnp.int32, (128, 128), 1)
    earlier = jnp.where((row // 16 == lane // 16) & (row < lane), 1.0, 0.0).astype(BF)
    first = (lax.broadcasted_iota(jnp.int32, (8, 128), 1) // 16) % 2 == 0
    keys = jnp.where(first, key2[0], key2[1])
    wts = jnp.where(first, wt2[0], wt2[1])

    def place(n, carry):
        r0 = pl.multiple_of(n * 128, 128)
        r = r0 + row
        expert = ((r // 16) * 2 + c).astype(F32)
        member = jnp.zeros((128, 128), F32)
        weight = jnp.zeros((128, 128), F32)
        for k in range(8):
            hit = jnp.abs(keys[k : k + 1, :] - expert) < 0.5
            member = jnp.where(hit, 1.0, member)
            weight = jnp.where(hit, wts[k : k + 1, :], weight)
        slot = mm(member.astype(BF), earlier) + (lane // 16 % 2 * 2).astype(F32)
        here = ((r // 4) % 4 == lane // 32) & (jnp.abs(slot - (r % 4).astype(F32)) < 0.5)
        one = jnp.where(here, member, 0.0)
        wsum = jnp.where(here, weight, 0.0)
        hi = wsum.astype(BF)
        lo = (wsum - hi.astype(F32)).astype(BF)
        m01[pl.ds(r0, 128), :] = one.astype(BF)
        mg[pl.ds(r0, 128), 0:128] = hi
        mg[pl.ds(r0, 128), 128:256] = lo
        one_t = jnp.transpose(one)
        w_t = jnp.transpose(wsum)
        hi_t = w_t.astype(BF)
        c01[:, pl.ds(r0, 128)] = one_t.astype(BF)
        cw[0:128, pl.ds(r0, 128)] = hi_t
        cw[128:256, pl.ds(r0, 128)] = (w_t - hi_t.astype(F32)).astype(BF)
        return carry

    lax.fori_loop(0, 8, place, 0)

    def some_units(src, dst, s_sem, r_sem, lo, count):
        def one(i, carry):
            d2, t2 = peer(lo + i)
            send(src.at[d2 * 8 + t2], dst.at[chip], s_sem, r_sem.at[chip // 16], (d2, t2 * 2 + c))
            return carry

        lax.fori_loop(0, count, one, 0)

    def scatter_units(src, dst, s_sem, r_sem, lo=1):
        some_units(src, dst, s_sem, r_sem, lo, CHIPS - lo)
        pltpu.make_async_copy(src.at[chip], dst.at[chip], r_sem.at[chip // 16]).start()

    def sent_units(src, s_sem):
        landed(src.at[pl.ds(0, CHIPS - 1)], s_sem)

    for h in range(2):
        landed(block(h), dg_r.at[h])

    def turn(i):
        return (z + i + i // 2 - i // 3 * 2) % 4

    def dense(i, carry):
        m = turn(i)
        landed(hid.at[m], hg_r.at[m])
        pf[m] = mm_t(jnp.transpose(hid[m]), down_t[...]).reshape(16, 16, quarter)

        def pack(t, carry):
            psend[m, t] = pf[m, 2 * t + 1 - c].astype(BF)
            return carry

        lax.fori_loop(0, 8, pack, 0)
        send(psend.at[m], prec.at[m], ps_s.at[m], ps_r.at[m], partner)
        return carry

    lax.fori_loop(0, 4, dense, 0)

    def reduce(i, carry):
        m = turn(i)
        landed(prec.at[m], ps_r.at[m])

        def add(t, carry):
            rs_send[m, t] = (pf[m, 2 * t + c] + prec[m, t].astype(F32)).astype(BF)
            return carry

        lax.fori_loop(0, 8, add, 0)

        def out(k, carry):
            t2 = ((tc // 4 + k // 4) % 2) * 4 + (y + k % 4) % 4
            send(rs_send.at[m, t2], rs_recv.at[m, tc], rs_s.at[m], rs_r.at[m], (dp, t2 * 2 + c))
            return carry

        lax.fori_loop(1, 8, out, 0)
        pltpu.make_async_copy(rs_send.at[m, tc], rs_recv.at[m, tc], rs_r.at[m]).start()
        return carry

    lax.fori_loop(0, 4, reduce, 0)

    for q in range(4):
        for b in range(2):
            part = cot2[b, :, q * quarter : (q + 1) * quarter]
            row = q * 32 + b * 16
            cg[row : row + 16, :] = part
            cg[128 + row : 128 + row + 16, :] = part

    def place_cot(g, carry):
        rows = mm(mg[pl.ds(pl.multiple_of(g * 256, 256), 256), :], cg[...])
        buf_a[pl.ds(g * 16, 16)] = rows.astype(BF).reshape(16, ROWS, quarter)
        return carry

    lax.fori_loop(0, 4, place_cot, 0)

    def cot_units(lo, count):
        some_units(buf_a, garr, ga_s, ga_r, lo, count)

    pl.semaphore_wait(space, 3)
    cot_units(1, COT[0])
    next_cot = 1 + COT[0]

    def sums_sent():
        def one(m, carry):
            landed(psend.at[m], ps_s.at[m])
            landed(rs_send.at[m, pl.ds(0, 7)], rs_s.at[m])
            return carry

        lax.fori_loop(0, 4, one, 0)

    pending.append(sums_sent)

    def to_owner(i, carry):
        m = turn(i)
        landed(rs_recv.at[m], rs_r.at[m])
        total = rs_recv[m, 0].astype(F32)
        for t in range(1, 8):
            total = total + rs_recv[m, t].astype(F32)
        zxs[m] = total

        @pl.when(i > 0)
        def _():
            send(zxs.at[m], zxr.at[z], zx_s.at[m], zx_r.at[z], (xh * 4 + m, tn))

        return carry

    lax.fori_loop(0, 4, to_owner, 0)
    cot_units(next_cot, COT[1])
    next_cot = next_cot + COT[1]
    pltpu.make_async_copy(zxs.at[z], zxr.at[z], zx_r.at[z]).start()

    def owner_sent():
        for k in range(1, 4):
            landed(zxs.at[0], zx_s.at[(z + k) % 4])

    pending.append(owner_sent)
    for m in range(4):
        landed(zxr.at[m], zx_r.at[m])
        for h in range(2):
            at = (4 * h + m) * half
            dense_f[:, at : at + half] = zxr[m, :, h * half : (h + 1) * half]
    st = (res[...].astype(F32) + dense_f[...]).astype(BF)
    stream[...] = st
    st = st.astype(F32)
    square = jnp.sum(st * st, axis=1, keepdims=True)
    inverse = lax.rsqrt(square / width + 1e-6)
    nrm2[c] = (stream[...].astype(F32) * inverse * gain[...].astype(F32)).astype(BF)
    nx = send(nrm2.at[c], nrm2.at[c], ex_s.at[3], ex_r.at[3], partner)
    nx.wait_recv()
    pending.append(nx.wait_send)

    for q in range(4):
        for b in range(2):
            row = q * 32 + b * 16
            cn[row : row + 16, :] = nrm2[b, :, q * quarter : (q + 1) * quarter]

    def place_nrm(g, carry):
        rows = mm(m01[pl.ds(pl.multiple_of(g * 256, 256), 256), :], cn[...])
        buf_b[pl.ds(g * 16, 16)] = rows.astype(BF).reshape(16, ROWS, quarter)
        return carry

    lax.fori_loop(0, 4, place_nrm, 0)
    scatter_units(buf_b, narr, na_s, na_r)
    scatter_units(buf_a, garr, ga_s, ga_r, next_cot)

    down2[...] = jnp.transpose(down_t[...])

    def collect(arr, r_sem):
        def group(g, carry):
            landed(arr.at[pl.ds(g * 16, 16)], r_sem.at[g])
            rows = mm(perm[...], arr[pl.ds(g * 16, 16)].reshape(256, quarter)).astype(BF)
            for q in range(4):
                xin[pl.ds(pl.multiple_of(g * 64, 64), 64), q * quarter : (q + 1) * quarter] = rows[
                    q * 64 : (q + 1) * 64
                ]
            return carry

        lax.fori_loop(0, 4, group, 0)

    collect(narr, na_r)
    load_wd.wait()
    load_wg.wait()
    load_wu.wait()

    def forward(n, carry):
        at = pl.ds(pl.multiple_of(n * 256, 256), 256)
        gate = mm(xin[...], wg[:, at])
        up = mm(xin[...], wu[:, at])
        gates[:, at] = gate
        ups[:, at] = up
        act[:, at] = (gate * jax.nn.sigmoid(gate) * up).astype(BF)
        return carry

    lax.fori_loop(0, 4, forward, 0)

    def backward(n, carry):
        at = pl.ds(pl.multiple_of(n * 256, 256), 256)
        ga = mm_t(xin[...], wd[at, :])
        gate = gates[:, at]
        s = jax.nn.sigmoid(gate)
        gg[:, at] = (ga * ups[:, at] * s * (1.0 + gate * (1.0 - s))).astype(BF)
        gu[:, at] = (ga * (gate * s)).astype(BF)
        return carry

    def to_zin(q, rows):
        rows = rows.astype(BF)
        for g in range(4):
            zin[g, pl.ds(pl.multiple_of(q * 64, 64), 64), :] = rows[g * 64 : (g + 1) * 64]

    def back_in(q, carry):
        at = pl.ds(pl.multiple_of(q * quarter, 128), quarter)
        to_zin(q, mm_t(gg[...], wg[at, :]) + mm_t(gu[...], wu[at, :]))
        return carry

    def from_zin(buf):
        def group(g, carry):
            rows = mm(perm_t[...], zin[g])
            buf[pl.ds(g * 16, 16)] = rows.astype(BF).reshape(16, ROWS, quarter)
            return carry

        lax.fori_loop(0, 4, group, 0)

    def down_out(q, carry):
        at = pl.ds(pl.multiple_of(q * quarter, 128), quarter)
        to_zin(q, mm(act[...], wd[:, at]))
        return carry

    def out_units(lo, count):
        some_units(buf_b, eret, ea_s, ea_r, lo, count)

    lax.fori_loop(0, 4, down_out, 0)
    sent_units(buf_b, na_s)
    from_zin(buf_b)
    out_units(1, OUT[0])
    collect(garr, ga_r)
    lax.fori_loop(0, 4, backward, 0)
    lax.fori_loop(0, 4, back_in, 0)
    sent_units(buf_a, ga_s)
    from_zin(buf_a)
    scatter_units(buf_a, hret, ha_s, ha_r)
    pending.append(lambda: sent_units(buf_a, ha_s))
    out_units(1 + OUT[0], OUT[1])
    next_out = 1 + OUT[0] + OUT[1]

    def share(u):
        def pack(q, carry):
            pax[u, q] = acc[u, 2 * q + 1 - c]
            return carry

        lax.fori_loop(0, 4, pack, 0)
        return send(pax.at[u], prx.at[u], px_s.at[u], px_r.at[u], partner)

    def summed(u, q):
        return acc[u, 2 * q + c] + prx[u, q]

    total = jnp.zeros((128, quarter), F32)
    for g in range(4):
        landed(hret.at[pl.ds(g * 16, 16)], ha_r.at[g])
        total = total + mm(c01[:, g * 256 : (g + 1) * 256], hret[g * 16 : (g + 1) * 16].reshape(256, quarter))
    acc[0] = total.reshape(8, 16, quarter)
    sh0 = share(0)
    sh0.wait_recv()
    pending.append(sh0.wait_send)

    dots = jnp.zeros((16, 1), F32)
    for q in range(4):
        cols = slice(q * quarter, (q + 1) * quarter)
        scaled = summed(0, q) * gain[:, cols].astype(F32)
        dots = dots + jnp.sum(scaled * (stream[:, cols].astype(F32) * inverse), axis=1, keepdims=True)
    mean = dots / width
    for q in range(4):
        cols = slice(q * quarter, (q + 1) * quarter)
        scaled = summed(0, q) * gain[:, cols].astype(F32)
        unit = stream[:, cols].astype(F32) * inverse
        gs_o[:, cols] = (cot[:, cols].astype(F32) + inverse * (scaled - unit * mean)).astype(BF)

    for m in range(4):
        for h in range(2):
            at = (4 * h + m) * half
            gsp[m, :, h * half : (h + 1) * half] = gs_o[:, at : at + half]
    for k in (2, 1, 3):
        to = (z + k) % 4
        pending.append(send(gsp.at[to], gs_all.at[tn, z], gx_s.at[k], gx_r.at[z], over_z[k]).wait_send)
    pltpu.make_async_copy(gsp.at[z], gs_all.at[tn, z], gx_r.at[z]).start()
    out_units(next_out, OUT[2])
    next_out2 = next_out + OUT[2]
    next_out2 = next_out + OUT[2]
    for n, k in enumerate((1, 3, 2, 0)):
        m = (z + k) % 4
        landed(gs_all.at[tn, m], gx_r.at[m])

        def gather_gs(i, carry):
            t2 = ((tc // 4 + i // 4) % 2) * 4 + (y + i % 4) % 4
            send(gs_all.at[tn, m], gs_all.at[tn, m], gs_s.at[m], gs_r.at[m, tc], (dp, t2 * 2 + c))
            return carry

        lax.fori_loop(1, 8, gather_gs, 0)
        send(gs_all.at[tn, m], gs_all.at[tn, m], fw_s.at[m], fw_r.at[m, tc], partner)
        out_units(next_out2 + n * OUT[3], OUT[3])

    for k in (1, 3, 2, 0):
        m = (z + k) % 4

        def forward_gs(i, carry):
            t2 = ((tc // 4 + i // 4) % 2) * 4 + (y + i % 4) % 4
            b2 = t2 * 2 + c
            landed(gs_all.at[b2, m], gs_r.at[m, t2])
            send(gs_all.at[b2, m], gs_all.at[b2, m], fw_s.at[m], fw_r.at[m, t2], partner)
            return carry

        lax.fori_loop(1, 8, forward_gs, 0)

        def all_gs(t, carry):
            landed(gs_all.at[t * 2 + 1 - c, m], fw_r.at[m, t])
            return carry

        lax.fori_loop(0, 8, all_gs, 0)
        gh = mm_t(down2[...], gs_all[:, m].reshape(256, quarter))
        if k:
            ghs[k] = gh.astype(BF)
            pending.append(send(ghs.at[k], ghr.at[z], gh_s.at[k], gh_r.at[z], over_z[k]).wait_send)

    def gs_sent():
        for m in range(4):
            landed(gs_all.at[pl.ds(0, 7), 0], gs_s.at[m])
            landed(gs_all.at[pl.ds(0, 8), 0], fw_s.at[m])

    pending.append(gs_sent)
    scatter_units(buf_b, eret, ea_s, ea_r, next_out2 + 4 * OUT[3])
    pending.append(lambda: sent_units(buf_b, ea_s))

    total = jnp.zeros((256, quarter), F32)
    for g in range(4):
        landed(eret.at[pl.ds(g * 16, 16)], ea_r.at[g])
        total = total + mm(cw[:, g * 256 : (g + 1) * 256], eret[g * 16 : (g + 1) * 16].reshape(256, quarter))
    acc[1] = (total[0:128] + total[128:256]).reshape(8, 16, quarter)
    sh1 = share(1)
    sh1.wait_recv()
    pending.append(sh1.wait_send)
    for q in range(4):
        cols = slice(q * quarter, (q + 1) * quarter)
        moe_o[:, cols] = (stream[:, cols].astype(F32) + summed(1, q)).astype(BF)

    for k in (1, 3, 2):
        at = (z + k) % 4
        landed(ghr.at[at], gh_r.at[at])
        gh = gh + ghr[at].astype(F32)
    gh_o[...] = gh.astype(BF)

    drain()


def hand_over(a, b, c, a_o, b_o, c_o):
    a_o[...] = a[...]
    b_o[...] = b[...]
    c_o[...] = c[...]


def body(
    dense_hidden, dense_down, residual, norm_gain, expert_ids, route_weights,
    w_gate, w_up, w_down, out_cotangent,
):
    width = residual.shape[1]
    q = width // 4
    hidden_units, cols = dense_down.shape
    fe = w_gate.shape[2]

    vmem = pl.BlockSpec(memory_space=pltpu.VMEM)
    hbm = pl.BlockSpec(memory_space=pl.ANY)
    V = pltpu.VMEM
    dma = pltpu.SemaphoreType.DMA
    unit = (CHIPS, ROWS, q)
    scratch = [
        V((4, hidden_units, 256), BF), V((2 * cols, hidden_units), BF), V((hidden_units, q), BF),
        V((width, fe), BF), V((width, fe), BF), V((fe, width), BF),
        V((1, width), BF), V((2, 16, width), BF), V((2, 8, 128), F32), V((2, 8, 128), F32), V((2, 16, width), BF),
        V((1024, 128), BF), V((1024, 256), BF), V((128, 1024), BF), V((256, 1024), BF),
        V((256, 256), BF), V((256, 256), BF), V((128, q), BF), V((256, q), BF),
        V(unit, BF), V(unit, BF), V(unit, BF), V(unit, BF), V(unit, BF), V(unit, BF),
        V((256, width), BF), V((256, fe), F32), V((256, fe), F32), V((256, fe), BF), V((256, fe), BF), V((256, fe), BF),
        V((4, 256, q), BF),
        V((4, 16, 16, q), F32), V((4, 8, 16, q), BF), V((4, 8, 16, q), BF), V((4, 8, 16, q), BF),
        V((4, 8, 16, q), BF), V((4, 16, q), F32), V((4, 16, q), F32), V((16, width), F32), V((16, width), BF),
        V((2, 8, 16, q), F32), V((2, 4, 16, q), F32), V((2, 4, 16, q), F32), V((4, 16, q), BF), V((16, 4, 16, q), BF),
        V((4, hidden_units, 256), BF), V((4, hidden_units, 256), BF),
        pltpu.SemaphoreType.REGULAR, pltpu.SemaphoreType.REGULAR,
        dma((4,)), dma((4,)), dma((4,)), dma((4,)), dma((4,)), dma, dma((2,)), dma((4,)), dma((4,)), dma((4,)), dma((4,)), dma((4,)), dma((4,)), dma((4,)), dma((4,)), dma((4,)), dma((4,)),
        dma, dma((4,)), dma, dma((4,)), dma, dma((4,)), dma, dma((4,)),
        dma((2,)), dma((2,)), dma((4,)), dma((4, 8)), dma((4,)), dma((4, 8)),
    ]
    moe, gs, gh = pl.pallas_call(
        kernel,
        out_shape=(
            jax.ShapeDtypeStruct(residual.shape, BF),
            jax.ShapeDtypeStruct(residual.shape, BF),
            jax.ShapeDtypeStruct(dense_hidden.shape[::-1], BF),
        ),
        in_specs=[hbm, hbm, vmem, vmem, vmem, vmem, vmem, hbm, hbm, hbm],
        out_specs=(vmem, vmem, vmem),
        scratch_shapes=scratch,
        compiler_params=pltpu.CompilerParams(
            collective_id=0, has_side_effects=True, vmem_limit_bytes=63 * 1024 * 1024
        ),
    )(
        dense_hidden.T, dense_down.T, residual, norm_gain, out_cotangent, expert_ids.T, route_weights.T,
        w_gate[0], w_up[0], w_down[0],
    )
    moe, gs, gh = pl.pallas_call(
        hand_over,
        out_shape=tuple(jax.ShapeDtypeStruct(a.shape, a.dtype) for a in (moe, gs, gh)),
        in_specs=[vmem] * 3,
        out_specs=(vmem,) * 3,
    )(moe, gs, gh)
    return moe, gs, gh.T


def solution(mesh):
    rows = P(("dp", "tensor"), None)
    experts = P(("dp", "tensor"), None, None)
    placed = (P("dp", "tensor"), P("tensor", "dp"), rows, P(), rows, rows, experts, experts, experts, rows)
    return jax.shard_map(
        body, mesh=mesh, in_specs=placed, out_specs=(rows, rows, P("dp", "tensor")), check_vma=False
    )
```

```python
import jax
import jax.numpy as jnp
from jax import lax
from jax.experimental import pallas as pl
from jax.experimental.pallas import tpu as pltpu
from jax.sharding import PartitionSpec as P

MESH = pl.DeviceIdType.MESH
BF = jnp.bfloat16
F32 = jnp.float32
CHIPS = 64
COT = (0, 26)
OUT = (36, 20, 4, 0)
ROWS = 16
NT = (((1,), (1,)), ((), ()))


def mm(a, b):
    return jnp.dot(a, b, preferred_element_type=F32)


def mm_t(a, b):
    return lax.dot_general(a, b, NT, preferred_element_type=F32)


def landed(ref, sem):
    pltpu.make_async_copy(ref, ref, sem).wait()


def kernel(
    hid_h, down_h, res, gain_in, cot, ids_in, wt_in, wg_h, wu_h, wd_h,
    moe_o, gs_o, gh_o,
    hid, down_t, down2, wg, wu, wd,
    gain, cot2, key2, wt2, nrm2,
    m01, mg, c01, cw, perm, perm_t, cn, cg,
    buf_a, garr, buf_b, narr, hret, eret,
    xin, gates, ups, act, gg, gu, zin,
    pf, psend, prec, rs_send, rs_recv, zxs, zxr, dense_f, stream,
    acc, pax, prx, gsp, gs_all, ghs, ghr,
    plane, space, loc, ex_s, ex_r, hg_s, hg_r, dg_s, dg_r, zx_s, zx_r, gx_s, gx_r, gh_s, gh_r, ps_s, ps_r, rs_s, rs_r,
    ga_s, ga_r, na_s, na_r, ha_s, ha_r, ea_s, ea_r, px_s, px_r, gs_s, gs_r, fw_s, fw_r,
):
    width = res.shape[1]
    quarter = width // 4
    half = quarter // 2
    dp = lax.axis_index("dp")
    tn = lax.axis_index("tensor")
    c = tn % 2
    tc = tn // 2
    chip = dp * 8 + tc
    z, y = dp % 4, tc % 4
    xh = dp // 4
    x = xh * 2 + tc // 4
    over_x = ((1 - xh) * 4 + z, tn)
    partner = (dp, tc * 2 + 1 - c)

    def peer(i):
        u = i // 4 % 4
        x2 = (x + i) % 4
        y2 = (y + i + u) % 4
        z2 = (z + i + 2 * u + i // 16) % 4
        return (x2 // 2) * 4 + z2, (x2 % 2) * 4 + y2

    def origin(i):
        u = i // 4 % 4
        x2 = (x + 3 * i) % 4
        y2 = (y + 3 * (i + u)) % 4
        z2 = (z + 3 * (i + 2 * u + i // 16)) % 4
        return (x2 // 2) * 4 + z2, (x2 % 2) * 4 + y2

    def send(src, dst, s_sem, r_sem, device):
        copy = pltpu.make_async_remote_copy(
            src_ref=src, dst_ref=dst, send_sem=s_sem, recv_sem=r_sem,
            device_id=device, device_id_type=MESH,
        )
        copy.start()
        return copy

    pending = []

    def drain():
        for done in pending:
            done()

    def block(h):
        return down_t.at[pl.ds(pl.multiple_of(h * half, 16), half)]

    pltpu.make_async_copy(down_h, block(xh), dg_r.at[xh]).start()
    pltpu.make_async_copy(hid_h, hid.at[z], hg_r.at[z]).start()
    load_wd = pltpu.make_async_copy(wd_h, wd, loc.at[1])
    load_wg = pltpu.make_async_copy(wg_h, wg, loc.at[2])
    load_wu = pltpu.make_async_copy(wu_h, wu, loc.at[3])

    barrier = pltpu.get_barrier_semaphore()

    def on_line(dx, dy, dz):
        x2, y2, z2 = (x + dx) % 4, (y + dy) % 4, (z + dz) % 4
        return (x2 // 2) * 4 + z2, ((x2 % 2) * 4 + y2) * 2 + c

    def signal(sem, to):
        pl.semaphore_signal(sem, inc=1, device_id=to, device_id_type=MESH)

    signal(barrier, partner)
    for k in (1, 2, 3):
        signal(barrier, on_line(0, 0, k))
        signal(barrier, on_line(k, 0, 0))
        signal(barrier, on_line(0, k, 0))

    lane = lax.broadcasted_iota(jnp.int32, (16, 128), 1)
    spread = jnp.where(lane % 16 == lax.broadcasted_iota(jnp.int32, (16, 128), 0), 1.0, 0.0)

    def lanes(a):
        return jnp.dot(a, spread, precision=lax.Precision.HIGHEST, preferred_element_type=F32)

    key2[c] = lanes(ids_in[...].astype(F32))
    wt2[c] = lanes(wt_in[...])
    cot2[c] = cot[...]
    gain[...] = gain_in[...].reshape(1, width)
    pl.semaphore_wait(barrier, 10)
    for k in (1, 2, 3):
        signal(plane, on_line(0, k, 0))

    ex = [
        send(key2.at[c], key2.at[c], ex_s.at[1], ex_r.at[1], partner),
        send(wt2.at[c], wt2.at[c], ex_s.at[2], ex_r.at[2], partner),
        send(cot2.at[c], cot2.at[c], ex_s.at[0], ex_r.at[0], partner),
    ]

    over_z = [(xh * 4 + (z + k) % 4, tn) for k in range(4)]
    pending.append(send(down_h, block(xh), dg_s, dg_r.at[xh], over_x).wait_send)
    for k in (1, 3, 2):
        pending.append(send(hid_h, hid.at[z], hg_s.at[k], hg_r.at[z], over_z[k]).wait_send)

    load_wg.start()
    load_wu.start()
    load_wd.start()

    pl.semaphore_wait(plane, 3)
    for k in (1, 2, 3):
        signal(space, on_line(0, 0, k))

    o = lax.broadcasted_iota(jnp.int32, (256, 256), 0)
    i = lax.broadcasted_iota(jnp.int32, (256, 256), 1)
    perm[...] = jnp.where((o % 64) // 4 * 16 + o // 64 * 4 + o % 4 == i, 1.0, 0.0).astype(BF)
    perm_t[...] = jnp.where((i % 64) // 4 * 16 + i // 64 * 4 + i % 4 == o, 1.0, 0.0).astype(BF)

    pending.extend(e.wait_send for e in ex)
    for e in ex:
        e.wait_recv()

    row = lax.broadcasted_iota(jnp.int32, (128, 128), 0)
    lane = lax.broadcasted_iota(jnp.int32, (128, 128), 1)
    earlier = jnp.where((row // 16 == lane // 16) & (row < lane), 1.0, 0.0).astype(BF)
    first = (lax.broadcasted_iota(jnp.int32, (8, 128), 1) // 16) % 2 == 0
    keys = jnp.where(first, key2[0], key2[1])
    wts = jnp.where(first, wt2[0], wt2[1])

    def place(n, carry):
        r0 = pl.multiple_of(n * 128, 128)
        r = r0 + row
        expert = ((r // 16) * 2 + c).astype(F32)
        member = jnp.zeros((128, 128), F32)
        weight = jnp.zeros((128, 128), F32)
        for k in range(8):
            hit = jnp.abs(keys[k : k + 1, :] - expert) < 0.5
            member = jnp.where(hit, 1.0, member)
            weight = jnp.where(hit, wts[k : k + 1, :], weight)
        slot = mm(member.astype(BF), earlier) + (lane // 16 % 2 * 2).astype(F32)
        here = ((r // 4) % 4 == lane // 32) & (jnp.abs(slot - (r % 4).astype(F32)) < 0.5)
        one = jnp.where(here, member, 0.0)
        wsum = jnp.where(here, weight, 0.0)
        hi = wsum.astype(BF)
        lo = (wsum - hi.astype(F32)).astype(BF)
        m01[pl.ds(r0, 128), :] = one.astype(BF)
        mg[pl.ds(r0, 128), 0:128] = hi
        mg[pl.ds(r0, 128), 128:256] = lo
        one_t = jnp.transpose(one)
        w_t = jnp.transpose(wsum)
        hi_t = w_t.astype(BF)
        c01[:, pl.ds(r0, 128)] = one_t.astype(BF)
        cw[0:128, pl.ds(r0, 128)] = hi_t
        cw[128:256, pl.ds(r0, 128)] = (w_t - hi_t.astype(F32)).astype(BF)
        return carry

    lax.fori_loop(0, 8, place, 0)

    def some_units(src, dst, s_sem, r_sem, lo, count):
        def one(i, carry):
            d2, t2 = peer(lo + i)
            send(src.at[d2 * 8 + t2], dst.at[lo + i], s_sem, r_sem.at[(lo + i) // 16], (d2, t2 * 2 + c))
            return carry

        lax.fori_loop(0, count, one, 0)

    def scatter_units(src, dst, s_sem, r_sem, lo=1):
        pltpu.make_async_copy(src.at[chip], dst.at[0], r_sem.at[0]).start()
        some_units(src, dst, s_sem, r_sem, lo, CHIPS - lo)

    def return_some(src, dst, s_sem, r_sem, lo, count):
        def one(i, carry):
            d2, t2 = origin(lo + i)
            send(src.at[lo + i], dst.at[chip], s_sem, r_sem.at[chip // 16], (d2, t2 * 2 + c))
            return carry

        lax.fori_loop(0, count, one, 0)

    def return_units(src, dst, s_sem, r_sem, lo=1):
        pltpu.make_async_copy(src.at[0], dst.at[chip], r_sem.at[chip // 16]).start()
        return_some(src, dst, s_sem, r_sem, lo, CHIPS - lo)

    def sent_units(src, s_sem):
        landed(src.at[pl.ds(0, CHIPS - 1)], s_sem)

    for h in range(2):
        landed(block(h), dg_r.at[h])

    def turn(i):
        return (z + i + i // 2 - i // 3 * 2) % 4

    def dense(i, carry):
        m = turn(i)
        landed(hid.at[m], hg_r.at[m])
        pf[m] = mm_t(jnp.transpose(hid[m]), down_t[...]).reshape(16, 16, quarter)

        def pack(t, carry):
            psend[m, t] = pf[m, 2 * t + 1 - c].astype(BF)
            return carry

        lax.fori_loop(0, 8, pack, 0)
        send(psend.at[m], prec.at[m], ps_s.at[m], ps_r.at[m], partner)
        return carry

    lax.fori_loop(0, 4, dense, 0)

    def reduce(i, carry):
        m = turn(i)
        landed(prec.at[m], ps_r.at[m])

        def add(t, carry):
            rs_send[m, t] = (pf[m, 2 * t + c] + prec[m, t].astype(F32)).astype(BF)
            return carry

        lax.fori_loop(0, 8, add, 0)

        def out(k, carry):
            t2 = ((tc // 4 + k // 4) % 2) * 4 + (y + k % 4) % 4
            send(rs_send.at[m, t2], rs_recv.at[m, tc], rs_s.at[m], rs_r.at[m], (dp, t2 * 2 + c))
            return carry

        lax.fori_loop(1, 8, out, 0)
        pltpu.make_async_copy(rs_send.at[m, tc], rs_recv.at[m, tc], rs_r.at[m]).start()
        return carry

    lax.fori_loop(0, 4, reduce, 0)

    for q in range(4):
        for b in range(2):
            part = cot2[b, :, q * quarter : (q + 1) * quarter]
            row = q * 32 + b * 16
            cg[row : row + 16, :] = part
            cg[128 + row : 128 + row + 16, :] = part

    def place_cot(g, carry):
        rows = mm(mg[pl.ds(pl.multiple_of(g * 256, 256), 256), :], cg[...])
        buf_a[pl.ds(g * 16, 16)] = rows.astype(BF).reshape(16, ROWS, quarter)
        return carry

    lax.fori_loop(0, 4, place_cot, 0)

    def cot_units(lo, count):
        some_units(buf_a, garr, ga_s, ga_r, lo, count)

    pl.semaphore_wait(space, 3)
    cot_units(1, COT[0])
    next_cot = 1 + COT[0]

    def sums_sent():
        def one(m, carry):
            landed(psend.at[m], ps_s.at[m])
            landed(rs_send.at[m, pl.ds(0, 7)], rs_s.at[m])
            return carry

        lax.fori_loop(0, 4, one, 0)

    pending.append(sums_sent)

    def to_owner(i, carry):
        m = turn(i)
        landed(rs_recv.at[m], rs_r.at[m])
        total = rs_recv[m, 0].astype(F32)
        for t in range(1, 8):
            total = total + rs_recv[m, t].astype(F32)
        zxs[m] = total

        @pl.when(i > 0)
        def _():
            send(zxs.at[m], zxr.at[z], zx_s.at[m], zx_r.at[z], (xh * 4 + m, tn))

        return carry

    lax.fori_loop(0, 4, to_owner, 0)
    cot_units(next_cot, COT[1])
    next_cot = next_cot + COT[1]
    pltpu.make_async_copy(zxs.at[z], zxr.at[z], zx_r.at[z]).start()

    def owner_sent():
        for k in range(1, 4):
            landed(zxs.at[0], zx_s.at[(z + k) % 4])

    pending.append(owner_sent)
    for m in range(4):
        landed(zxr.at[m], zx_r.at[m])
        for h in range(2):
            at = (4 * h + m) * half
            dense_f[:, at : at + half] = zxr[m, :, h * half : (h + 1) * half]
    st = (res[...].astype(F32) + dense_f[...]).astype(BF)
    stream[...] = st
    st = st.astype(F32)
    square = jnp.sum(st * st, axis=1, keepdims=True)
    inverse = lax.rsqrt(square / width + 1e-6)
    nrm2[c] = (stream[...].astype(F32) * inverse * gain[...].astype(F32)).astype(BF)
    nx = send(nrm2.at[c], nrm2.at[c], ex_s.at[3], ex_r.at[3], partner)
    nx.wait_recv()
    pending.append(nx.wait_send)

    for q in range(4):
        for b in range(2):
            row = q * 32 + b * 16
            cn[row : row + 16, :] = nrm2[b, :, q * quarter : (q + 1) * quarter]

    def place_nrm(g, carry):
        rows = mm(m01[pl.ds(pl.multiple_of(g * 256, 256), 256), :], cn[...])
        buf_b[pl.ds(g * 16, 16)] = rows.astype(BF).reshape(16, ROWS, quarter)
        return carry

    lax.fori_loop(0, 4, place_nrm, 0)
    scatter_units(buf_b, narr, na_s, na_r)
    scatter_units(buf_a, garr, ga_s, ga_r, next_cot)

    down2[...] = jnp.transpose(down_t[...])

    def collect(arr, r_sem):
        def group(g, carry):
            landed(arr.at[pl.ds(g * 16, 16)], r_sem.at[g])
            rows = mm(perm[...], arr[pl.ds(g * 16, 16)].reshape(256, quarter)).astype(BF)
            for q in range(4):
                xin[pl.ds(pl.multiple_of(g * 64, 64), 64), q * quarter : (q + 1) * quarter] = rows[
                    q * 64 : (q + 1) * 64
                ]
            return carry

        lax.fori_loop(0, 4, group, 0)

    collect(narr, na_r)
    load_wd.wait()
    load_wg.wait()
    load_wu.wait()

    def forward(n, carry):
        at = pl.ds(pl.multiple_of(n * 256, 256), 256)
        gate = mm(xin[...], wg[:, at])
        up = mm(xin[...], wu[:, at])
        gates[:, at] = gate
        ups[:, at] = up
        act[:, at] = (gate * jax.nn.sigmoid(gate) * up).astype(BF)
        return carry

    lax.fori_loop(0, 4, forward, 0)

    def backward(n, carry):
        at = pl.ds(pl.multiple_of(n * 256, 256), 256)
        ga = mm_t(xin[...], wd[at, :])
        gate = gates[:, at]
        s = jax.nn.sigmoid(gate)
        gg[:, at] = (ga * ups[:, at] * s * (1.0 + gate * (1.0 - s))).astype(BF)
        gu[:, at] = (ga * (gate * s)).astype(BF)
        return carry

    def to_zin(q, rows):
        rows = rows.astype(BF)
        for g in range(4):
            zin[g, pl.ds(pl.multiple_of(q * 64, 64), 64), :] = rows[g * 64 : (g + 1) * 64]

    def back_in(q, carry):
        at = pl.ds(pl.multiple_of(q * quarter, 128), quarter)
        to_zin(q, mm_t(gg[...], wg[at, :]) + mm_t(gu[...], wu[at, :]))
        return carry

    def from_zin(buf):
        def group(g, carry):
            rows = mm(perm_t[...], zin[g])
            buf[pl.ds(g * 16, 16)] = rows.astype(BF).reshape(16, ROWS, quarter)
            return carry

        lax.fori_loop(0, 4, group, 0)

    def down_out(q, carry):
        at = pl.ds(pl.multiple_of(q * quarter, 128), quarter)
        to_zin(q, mm(act[...], wd[:, at]))
        return carry

    def out_units(lo, count):
        return_some(buf_b, eret, ea_s, ea_r, lo, count)

    lax.fori_loop(0, 4, down_out, 0)
    sent_units(buf_b, na_s)
    from_zin(buf_b)
    out_units(1, OUT[0])
    collect(garr, ga_r)
    lax.fori_loop(0, 4, backward, 0)
    lax.fori_loop(0, 4, back_in, 0)
    sent_units(buf_a, ga_s)
    from_zin(buf_a)
    return_units(buf_a, hret, ha_s, ha_r)
    pending.append(lambda: sent_units(buf_a, ha_s))
    out_units(1 + OUT[0], OUT[1])
    next_out = 1 + OUT[0] + OUT[1]

    def share(u):
        def pack(q, carry):
            pax[u, q] = acc[u, 2 * q + 1 - c]
            return carry

        lax.fori_loop(0, 4, pack, 0)
        return send(pax.at[u], prx.at[u], px_s.at[u], px_r.at[u], partner)

    def summed(u, q):
        return acc[u, 2 * q + c] + prx[u, q]

    total = jnp.zeros((128, quarter), F32)
    for g in range(4):
        landed(hret.at[pl.ds(g * 16, 16)], ha_r.at[g])
        total = total + mm(c01[:, g * 256 : (g + 1) * 256], hret[g * 16 : (g + 1) * 16].reshape(256, quarter))
    acc[0] = total.reshape(8, 16, quarter)
    sh0 = share(0)
    sh0.wait_recv()
    pending.append(sh0.wait_send)

    dots = jnp.zeros((16, 1), F32)
    for q in range(4):
        cols = slice(q * quarter, (q + 1) * quarter)
        scaled = summed(0, q) * gain[:, cols].astype(F32)
        dots = dots + jnp.sum(scaled * (stream[:, cols].astype(F32) * inverse), axis=1, keepdims=True)
    mean = dots / width
    for q in range(4):
        cols = slice(q * quarter, (q + 1) * quarter)
        scaled = summed(0, q) * gain[:, cols].astype(F32)
        unit = stream[:, cols].astype(F32) * inverse
        gs_o[:, cols] = (cot[:, cols].astype(F32) + inverse * (scaled - unit * mean)).astype(BF)

    for m in range(4):
        for h in range(2):
            at = (4 * h + m) * half
            gsp[m, :, h * half : (h + 1) * half] = gs_o[:, at : at + half]
    for k in (2, 1, 3):
        to = (z + k) % 4
        pending.append(send(gsp.at[to], gs_all.at[tn, z], gx_s.at[k], gx_r.at[z], over_z[k]).wait_send)
    pltpu.make_async_copy(gsp.at[z], gs_all.at[tn, z], gx_r.at[z]).start()
    out_units(next_out, OUT[2])
    next_out2 = next_out + OUT[2]
    next_out2 = next_out + OUT[2]
    for n, k in enumerate((1, 3, 2, 0)):
        m = (z + k) % 4
        landed(gs_all.at[tn, m], gx_r.at[m])

        def gather_gs(i, carry):
            t2 = ((tc // 4 + i // 4) % 2) * 4 + (y + i % 4) % 4
            send(gs_all.at[tn, m], gs_all.at[tn, m], gs_s.at[m], gs_r.at[m, tc], (dp, t2 * 2 + c))
            return carry

        lax.fori_loop(1, 8, gather_gs, 0)
        send(gs_all.at[tn, m], gs_all.at[tn, m], fw_s.at[m], fw_r.at[m, tc], partner)
        out_units(next_out2 + n * OUT[3], OUT[3])

    for k in (1, 3, 2, 0):
        m = (z + k) % 4

        def forward_gs(i, carry):
            t2 = ((tc // 4 + i // 4) % 2) * 4 + (y + i % 4) % 4
            b2 = t2 * 2 + c
            landed(gs_all.at[b2, m], gs_r.at[m, t2])
            send(gs_all.at[b2, m], gs_all.at[b2, m], fw_s.at[m], fw_r.at[m, t2], partner)
            return carry

        lax.fori_loop(1, 8, forward_gs, 0)

        def all_gs(t, carry):
            landed(gs_all.at[t * 2 + 1 - c, m], fw_r.at[m, t])
            return carry

        lax.fori_loop(0, 8, all_gs, 0)
        gh = mm_t(down2[...], gs_all[:, m].reshape(256, quarter))
        if k:
            ghs[k] = gh.astype(BF)
            pending.append(send(ghs.at[k], ghr.at[z], gh_s.at[k], gh_r.at[z], over_z[k]).wait_send)

    def gs_sent():
        for m in range(4):
            landed(gs_all.at[pl.ds(0, 7), 0], gs_s.at[m])
            landed(gs_all.at[pl.ds(0, 8), 0], fw_s.at[m])

    pending.append(gs_sent)
    return_units(buf_b, eret, ea_s, ea_r, next_out2 + 4 * OUT[3])
    pending.append(lambda: sent_units(buf_b, ea_s))

    total = jnp.zeros((256, quarter), F32)
    for g in range(4):
        landed(eret.at[pl.ds(g * 16, 16)], ea_r.at[g])
        total = total + mm(cw[:, g * 256 : (g + 1) * 256], eret[g * 16 : (g + 1) * 16].reshape(256, quarter))
    acc[1] = (total[0:128] + total[128:256]).reshape(8, 16, quarter)
    sh1 = share(1)
    sh1.wait_recv()
    pending.append(sh1.wait_send)
    for q in range(4):
        cols = slice(q * quarter, (q + 1) * quarter)
        moe_o[:, cols] = (stream[:, cols].astype(F32) + summed(1, q)).astype(BF)

    for k in (1, 3, 2):
        at = (z + k) % 4
        landed(ghr.at[at], gh_r.at[at])
        gh = gh + ghr[at].astype(F32)
    gh_o[...] = gh.astype(BF)

    drain()


def hand_over(a, b, c, a_o, b_o, c_o):
    a_o[...] = a[...]
    b_o[...] = b[...]
    c_o[...] = c[...]


def body(
    dense_hidden, dense_down, residual, norm_gain, expert_ids, route_weights,
    w_gate, w_up, w_down, out_cotangent,
):
    width = residual.shape[1]
    q = width // 4
    hidden_units, cols = dense_down.shape
    fe = w_gate.shape[2]

    vmem = pl.BlockSpec(memory_space=pltpu.VMEM)
    hbm = pl.BlockSpec(memory_space=pl.ANY)
    V = pltpu.VMEM
    dma = pltpu.SemaphoreType.DMA
    unit = (CHIPS, ROWS, q)
    scratch = [
        V((4, hidden_units, 256), BF), V((2 * cols, hidden_units), BF), V((hidden_units, q), BF),
        V((width, fe), BF), V((width, fe), BF), V((fe, width), BF),
        V((1, width), BF), V((2, 16, width), BF), V((2, 8, 128), F32), V((2, 8, 128), F32), V((2, 16, width), BF),
        V((1024, 128), BF), V((1024, 256), BF), V((128, 1024), BF), V((256, 1024), BF),
        V((256, 256), BF), V((256, 256), BF), V((128, q), BF), V((256, q), BF),
        V(unit, BF), V(unit, BF), V(unit, BF), V(unit, BF), V(unit, BF), V(unit, BF),
        V((256, width), BF), V((256, fe), F32), V((256, fe), F32), V((256, fe), BF), V((256, fe), BF), V((256, fe), BF),
        V((4, 256, q), BF),
        V((4, 16, 16, q), F32), V((4, 8, 16, q), BF), V((4, 8, 16, q), BF), V((4, 8, 16, q), BF),
        V((4, 8, 16, q), BF), V((4, 16, q), F32), V((4, 16, q), F32), V((16, width), F32), V((16, width), BF),
        V((2, 8, 16, q), F32), V((2, 4, 16, q), F32), V((2, 4, 16, q), F32), V((4, 16, q), BF), V((16, 4, 16, q), BF),
        V((4, hidden_units, 256), BF), V((4, hidden_units, 256), BF),
        pltpu.SemaphoreType.REGULAR, pltpu.SemaphoreType.REGULAR,
        dma((4,)), dma((4,)), dma((4,)), dma((4,)), dma((4,)), dma, dma((2,)), dma((4,)), dma((4,)), dma((4,)), dma((4,)), dma((4,)), dma((4,)), dma((4,)), dma((4,)), dma((4,)), dma((4,)),
        dma, dma((4,)), dma, dma((4,)), dma, dma((4,)), dma, dma((4,)),
        dma((2,)), dma((2,)), dma((4,)), dma((4, 8)), dma((4,)), dma((4, 8)),
    ]
    moe, gs, gh = pl.pallas_call(
        kernel,
        out_shape=(
            jax.ShapeDtypeStruct(residual.shape, BF),
            jax.ShapeDtypeStruct(residual.shape, BF),
            jax.ShapeDtypeStruct(dense_hidden.shape[::-1], BF),
        ),
        in_specs=[hbm, hbm, vmem, vmem, vmem, vmem, vmem, hbm, hbm, hbm],
        out_specs=(vmem, vmem, vmem),
        scratch_shapes=scratch,
        compiler_params=pltpu.CompilerParams(
            collective_id=0, has_side_effects=True, vmem_limit_bytes=63 * 1024 * 1024
        ),
    )(
        dense_hidden.T, dense_down.T, residual, norm_gain, out_cotangent, expert_ids.T, route_weights.T,
        w_gate[0], w_up[0], w_down[0],
    )
    moe, gs, gh = pl.pallas_call(
        hand_over,
        out_shape=tuple(jax.ShapeDtypeStruct(a.shape, a.dtype) for a in (moe, gs, gh)),
        in_specs=[vmem] * 3,
        out_specs=(vmem,) * 3,
    )(moe, gs, gh)
    return moe, gs, gh.T


def solution(mesh):
    rows = P(("dp", "tensor"), None)
    experts = P(("dp", "tensor"), None, None)
    placed = (P("dp", "tensor"), P("tensor", "dp"), rows, P(), rows, rows, experts, experts, experts, rows)
    return jax.shard_map(
        body, mesh=mesh, in_specs=placed, out_specs=(rows, rows, P("dp", "tensor")), check_vma=False
    )
```

```python
import jax
import jax.numpy as jnp
from jax import lax
from jax.experimental import pallas as pl
from jax.experimental.pallas import tpu as pltpu
from jax.sharding import PartitionSpec as P

MESH = pl.DeviceIdType.MESH
BF = jnp.bfloat16
F32 = jnp.float32
CHIPS = 64
COT = (0, 26)
OUT = (36, 20, 4, 0)
ROWS = 16
NT = (((1,), (1,)), ((), ()))


def mm(a, b):
    return jnp.dot(a, b, preferred_element_type=F32)


def mm_t(a, b):
    return lax.dot_general(a, b, NT, preferred_element_type=F32)


def landed(ref, sem):
    pltpu.make_async_copy(ref, ref, sem).wait()


def kernel(
    hid_h, down_h, res, gain_in, cot, ids_in, wt_in, wg_h, wu_h, wd_h,
    moe_o, gs_o, gh_o,
    hid, down_t, down2, wg, wu, wd,
    gain, cot2, key2, wt2, nrm2,
    m01, mg, c01, cw, perm, perm_t, cn, cg,
    buf_a, garr, buf_b, narr, hret, eret,
    xin, gates, ups, act, gg, gu, zin,
    pf, psend, prec, rs_send, rs_recv, zxs, zxr, dense_f, stream,
    acc, pax, prx, gsp, gs_all, ghs, ghr,
    plane, space, loc, ex_s, ex_r, hg_s, hg_r, dg_s, dg_r, zx_s, zx_r, gx_s, gx_r, gh_s, gh_r, ps_s, ps_r, rs_s, rs_r,
    ga_s, ga_r, na_s, na_r, ha_s, ha_r, ea_s, ea_r, px_s, px_r, gs_s, gs_r, fw_s, fw_r,
):
    width = res.shape[1]
    quarter = width // 4
    half = quarter // 2
    dp = lax.axis_index("dp")
    tn = lax.axis_index("tensor")
    c = tn % 2
    tc = tn // 2
    chip = dp * 8 + tc
    z, y = dp % 4, tc % 4
    xh = dp // 4
    x = xh * 2 + tc // 4
    over_x = ((1 - xh) * 4 + z, tn)
    partner = (dp, tc * 2 + 1 - c)

    def peer(i):
        u = i // 4 % 4
        x2 = (x + i) % 4
        y2 = (y + i + u) % 4
        z2 = (z + i + 2 * u + i // 16) % 4
        return (x2 // 2) * 4 + z2, (x2 % 2) * 4 + y2

    def origin(i):
        u = i // 4 % 4
        x2 = (x + 3 * i) % 4
        y2 = (y + 3 * (i + u)) % 4
        z2 = (z + 3 * (i + 2 * u + i // 16)) % 4
        return (x2 // 2) * 4 + z2, (x2 % 2) * 4 + y2

    def send(src, dst, s_sem, r_sem, device):
        copy = pltpu.make_async_remote_copy(
            src_ref=src, dst_ref=dst, send_sem=s_sem, recv_sem=r_sem,
            device_id=device, device_id_type=MESH,
        )
        copy.start()
        return copy

    pending = []

    def drain():
        for done in pending:
            done()

    def block(h):
        return down_t.at[pl.ds(pl.multiple_of(h * half, 16), half)]

    pltpu.make_async_copy(down_h, block(xh), dg_r.at[xh]).start()
    pltpu.make_async_copy(hid_h, hid.at[z], hg_r.at[z]).start()
    load_wd = pltpu.make_async_copy(wd_h, wd, loc.at[1])
    load_wg = pltpu.make_async_copy(wg_h, wg, loc.at[2])
    load_wu = pltpu.make_async_copy(wu_h, wu, loc.at[3])

    barrier = pltpu.get_barrier_semaphore()

    def on_line(dx, dy, dz):
        x2, y2, z2 = (x + dx) % 4, (y + dy) % 4, (z + dz) % 4
        return (x2 // 2) * 4 + z2, ((x2 % 2) * 4 + y2) * 2 + c

    def signal(sem, to):
        pl.semaphore_signal(sem, inc=1, device_id=to, device_id_type=MESH)

    signal(barrier, partner)
    for k in (1, 2, 3):
        signal(barrier, on_line(0, 0, k))
        signal(barrier, on_line(k, 0, 0))
        signal(barrier, on_line(0, k, 0))

    lane = lax.broadcasted_iota(jnp.int32, (16, 128), 1)
    spread = jnp.where(lane % 16 == lax.broadcasted_iota(jnp.int32, (16, 128), 0), 1.0, 0.0)

    def lanes(a):
        return jnp.dot(a, spread, precision=lax.Precision.HIGHEST, preferred_element_type=F32)

    key2[c] = lanes(ids_in[...].astype(F32))
    wt2[c] = lanes(wt_in[...])
    cot2[c] = cot[...]
    gain[...] = gain_in[...].reshape(1, width)
    pl.semaphore_wait(barrier, 10)
    for k in (1, 2, 3):
        signal(plane, on_line(0, k, 0))

    ex = [
        send(key2.at[c], key2.at[c], ex_s.at[1], ex_r.at[1], partner),
        send(wt2.at[c], wt2.at[c], ex_s.at[2], ex_r.at[2], partner),
        send(cot2.at[c], cot2.at[c], ex_s.at[0], ex_r.at[0], partner),
    ]

    over_z = [(xh * 4 + (z + k) % 4, tn) for k in range(4)]
    pending.append(send(down_h, block(xh), dg_s, dg_r.at[xh], over_x).wait_send)
    for k in (1, 3, 2):
        pending.append(send(hid_h, hid.at[z], hg_s.at[k], hg_r.at[z], over_z[k]).wait_send)

    load_wg.start()
    load_wu.start()
    load_wd.start()

    pl.semaphore_wait(plane, 3)
    for k in (1, 2, 3):
        signal(space, on_line(0, 0, k))

    o = lax.broadcasted_iota(jnp.int32, (256, 256), 0)
    i = lax.broadcasted_iota(jnp.int32, (256, 256), 1)
    perm[...] = jnp.where((o % 64) // 4 * 16 + o // 64 * 4 + o % 4 == i, 1.0, 0.0).astype(BF)
    perm_t[...] = jnp.where((i % 64) // 4 * 16 + i // 64 * 4 + i % 4 == o, 1.0, 0.0).astype(BF)

    pending.extend(e.wait_send for e in ex)
    for e in ex:
        e.wait_recv()

    row = lax.broadcasted_iota(jnp.int32, (128, 128), 0)
    lane = lax.broadcasted_iota(jnp.int32, (128, 128), 1)
    earlier = jnp.where((row // 16 == lane // 16) & (row < lane), 1.0, 0.0).astype(BF)
    first = (lax.broadcasted_iota(jnp.int32, (8, 128), 1) // 16) % 2 == 0
    keys = jnp.where(first, key2[0], key2[1])
    wts = jnp.where(first, wt2[0], wt2[1])

    def place(n, carry):
        r0 = pl.multiple_of(n * 128, 128)
        r = r0 + row
        expert = ((r // 16) * 2 + c).astype(F32)
        member = jnp.zeros((128, 128), F32)
        weight = jnp.zeros((128, 128), F32)
        for k in range(8):
            hit = jnp.abs(keys[k : k + 1, :] - expert) < 0.5
            member = jnp.where(hit, 1.0, member)
            weight = jnp.where(hit, wts[k : k + 1, :], weight)
        slot = mm(member.astype(BF), earlier) + (lane // 16 % 2 * 2).astype(F32)
        here = ((r // 4) % 4 == lane // 32) & (jnp.abs(slot - (r % 4).astype(F32)) < 0.5)
        one = jnp.where(here, member, 0.0)
        wsum = jnp.where(here, weight, 0.0)
        hi = wsum.astype(BF)
        lo = (wsum - hi.astype(F32)).astype(BF)
        m01[pl.ds(r0, 128), :] = one.astype(BF)
        mg[pl.ds(r0, 128), 0:128] = hi
        mg[pl.ds(r0, 128), 128:256] = lo
        one_t = jnp.transpose(one)
        w_t = jnp.transpose(wsum)
        hi_t = w_t.astype(BF)
        c01[:, pl.ds(r0, 128)] = one_t.astype(BF)
        cw[0:128, pl.ds(r0, 128)] = hi_t
        cw[128:256, pl.ds(r0, 128)] = (w_t - hi_t.astype(F32)).astype(BF)
        return carry

    lax.fori_loop(0, 8, place, 0)

    def some_units(src, dst, s_sem, r_sem, lo, count):
        def one(i, carry):
            d2, t2 = peer(lo + i)
            send(src.at[d2 * 8 + t2], dst.at[lo + i], s_sem, r_sem.at[(lo + i) // 16], (d2, t2 * 2 + c))
            return carry

        lax.fori_loop(0, count, one, 0)

    def scatter_units(src, dst, s_sem, r_sem, lo=1):
        pltpu.make_async_copy(src.at[chip], dst.at[0], r_sem.at[0]).start()
        some_units(src, dst, s_sem, r_sem, lo, CHIPS - lo)

    def return_some(src, dst, s_sem, r_sem, lo, count):
        def one(i, carry):
            d2, t2 = origin(lo + i)
            send(src.at[lo + i], dst.at[chip], s_sem, r_sem.at[chip // 16], (d2, t2 * 2 + c))
            return carry

        lax.fori_loop(0, count, one, 0)

    def return_units(src, dst, s_sem, r_sem, lo=1):
        pltpu.make_async_copy(src.at[0], dst.at[chip], r_sem.at[chip // 16]).start()
        return_some(src, dst, s_sem, r_sem, lo, CHIPS - lo)

    def sent_units(src, s_sem):
        landed(src.at[pl.ds(0, CHIPS - 1)], s_sem)

    for h in range(2):
        landed(block(h), dg_r.at[h])

    def turn(i):
        return (z + i + i // 2 - i // 3 * 2) % 4

    def dense(i, carry):
        m = turn(i)
        landed(hid.at[m], hg_r.at[m])
        pf[m] = mm_t(jnp.transpose(hid[m]), down_t[...]).reshape(16, 16, quarter)

        def pack(t, carry):
            psend[m, t] = pf[m, 2 * t + 1 - c].astype(BF)
            return carry

        lax.fori_loop(0, 8, pack, 0)
        send(psend.at[m], prec.at[m], ps_s.at[m], ps_r.at[m], partner)
        return carry

    lax.fori_loop(0, 4, dense, 0)

    def reduce(i, carry):
        m = turn(i)
        landed(prec.at[m], ps_r.at[m])

        def add(t, carry):
            rs_send[m, t] = (pf[m, 2 * t + c] + prec[m, t].astype(F32)).astype(BF)
            return carry

        lax.fori_loop(0, 8, add, 0)

        def out(k, carry):
            t2 = ((tc // 4 + k // 4) % 2) * 4 + (y + k % 4) % 4
            send(rs_send.at[m, t2], rs_recv.at[m, tc], rs_s.at[m], rs_r.at[m], (dp, t2 * 2 + c))
            return carry

        lax.fori_loop(1, 8, out, 0)
        pltpu.make_async_copy(rs_send.at[m, tc], rs_recv.at[m, tc], rs_r.at[m]).start()
        return carry

    lax.fori_loop(0, 4, reduce, 0)

    for q in range(4):
        for b in range(2):
            part = cot2[b, :, q * quarter : (q + 1) * quarter]
            row = q * 32 + b * 16
            cg[row : row + 16, :] = part
            cg[128 + row : 128 + row + 16, :] = part

    def place_cot(g, carry):
        rows = mm(mg[pl.ds(pl.multiple_of(g * 256, 256), 256), :], cg[...])
        buf_a[pl.ds(g * 16, 16)] = rows.astype(BF).reshape(16, ROWS, quarter)
        return carry

    lax.fori_loop(0, 4, place_cot, 0)

    def cot_units(lo, count):
        some_units(buf_a, garr, ga_s, ga_r, lo, count)

    pl.semaphore_wait(space, 3)
    cot_units(1, COT[0])
    next_cot = 1 + COT[0]

    def sums_sent():
        def one(m, carry):
            landed(psend.at[m], ps_s.at[m])
            landed(rs_send.at[m, pl.ds(0, 7)], rs_s.at[m])
            return carry

        lax.fori_loop(0, 4, one, 0)

    pending.append(sums_sent)

    def to_owner(i, carry):
        m = turn(i)
        landed(rs_recv.at[m], rs_r.at[m])
        total = rs_recv[m, 0].astype(F32)
        for t in range(1, 8):
            total = total + rs_recv[m, t].astype(F32)
        zxs[m] = total

        @pl.when(i > 0)
        def _():
            send(zxs.at[m], zxr.at[z], zx_s.at[m], zx_r.at[z], (xh * 4 + m, tn))

        return carry

    lax.fori_loop(0, 4, to_owner, 0)
    cot_units(next_cot, COT[1])
    next_cot = next_cot + COT[1]
    pltpu.make_async_copy(zxs.at[z], zxr.at[z], zx_r.at[z]).start()

    def owner_sent():
        for k in range(1, 4):
            landed(zxs.at[0], zx_s.at[(z + k) % 4])

    pending.append(owner_sent)
    for m in range(4):
        landed(zxr.at[m], zx_r.at[m])
        for h in range(2):
            at = (4 * h + m) * half
            dense_f[:, at : at + half] = zxr[m, :, h * half : (h + 1) * half]
    st = (res[...].astype(F32) + dense_f[...]).astype(BF)
    stream[...] = st
    st = st.astype(F32)
    square = jnp.sum(st * st, axis=1, keepdims=True)
    inverse = lax.rsqrt(square / width + 1e-6)
    nrm2[c] = (stream[...].astype(F32) * inverse * gain[...].astype(F32)).astype(BF)
    nx = send(nrm2.at[c], nrm2.at[c], ex_s.at[3], ex_r.at[3], partner)
    nx.wait_recv()
    pending.append(nx.wait_send)

    for q in range(4):
        for b in range(2):
            row = q * 32 + b * 16
            cn[row : row + 16, :] = nrm2[b, :, q * quarter : (q + 1) * quarter]

    def place_nrm(g, carry):
        rows = mm(m01[pl.ds(pl.multiple_of(g * 256, 256), 256), :], cn[...])
        buf_b[pl.ds(g * 16, 16)] = rows.astype(BF).reshape(16, ROWS, quarter)
        return carry

    lax.fori_loop(0, 4, place_nrm, 0)
    scatter_units(buf_b, narr, na_s, na_r)
    scatter_units(buf_a, garr, ga_s, ga_r, next_cot)

    down2[...] = jnp.transpose(down_t[...])

    def collect(arr, r_sem):
        def group(g, carry):
            landed(arr.at[pl.ds(g * 16, 16)], r_sem.at[g])
            rows = mm(perm[...], arr[pl.ds(g * 16, 16)].reshape(256, quarter)).astype(BF)
            for q in range(4):
                xin[pl.ds(pl.multiple_of(g * 64, 64), 64), q * quarter : (q + 1) * quarter] = rows[
                    q * 64 : (q + 1) * 64
                ]
            return carry

        lax.fori_loop(0, 4, group, 0)

    collect(narr, na_r)
    load_wd.wait()
    load_wg.wait()
    load_wu.wait()

    def forward(n, carry):
        at = pl.ds(pl.multiple_of(n * 256, 256), 256)
        gate = mm(xin[...], wg[:, at])
        up = mm(xin[...], wu[:, at])
        gates[:, at] = gate
        ups[:, at] = up
        act[:, at] = (gate * jax.nn.sigmoid(gate) * up).astype(BF)
        return carry

    lax.fori_loop(0, 4, forward, 0)

    def backward(n, carry):
        at = pl.ds(pl.multiple_of(n * 256, 256), 256)
        ga = mm_t(xin[...], wd[at, :])
        gate = gates[:, at]
        s = jax.nn.sigmoid(gate)
        gg[:, at] = (ga * ups[:, at] * s * (1.0 + gate * (1.0 - s))).astype(BF)
        gu[:, at] = (ga * (gate * s)).astype(BF)
        return carry

    def to_zin(q, rows):
        rows = rows.astype(BF)
        for g in range(4):
            zin[g, pl.ds(pl.multiple_of(q * 64, 64), 64), :] = rows[g * 64 : (g + 1) * 64]

    def back_in(q, carry):
        at = pl.ds(pl.multiple_of(q * quarter, 128), quarter)
        to_zin(q, mm_t(gg[...], wg[at, :]) + mm_t(gu[...], wu[at, :]))
        return carry

    def from_zin(buf):
        def group(g, carry):
            rows = mm(perm_t[...], zin[g])
            buf[pl.ds(g * 16, 16)] = rows.astype(BF).reshape(16, ROWS, quarter)
            return carry

        lax.fori_loop(0, 4, group, 0)

    def down_out(q, carry):
        at = pl.ds(pl.multiple_of(q * quarter, 128), quarter)
        to_zin(q, mm(act[...], wd[:, at]))
        return carry

    def out_units(lo, count):
        return_some(buf_b, eret, ea_s, ea_r, lo, count)

    lax.fori_loop(0, 4, down_out, 0)
    sent_units(buf_b, na_s)
    from_zin(buf_b)
    out_units(1, OUT[0])
    collect(garr, ga_r)
    lax.fori_loop(0, 4, backward, 0)
    lax.fori_loop(0, 4, back_in, 0)
    sent_units(buf_a, ga_s)
    for g in range(4):
        buf_a[g * 16 : (g + 1) * 16] = mm(perm_t[...], zin[g]).astype(BF).reshape(16, ROWS, quarter)
        return_some(buf_a, hret, ha_s, ha_r, max(g * 16, 1), 16 if g else 15)
    pltpu.make_async_copy(buf_a.at[0], hret.at[chip], ha_r.at[chip // 16]).start()
    pending.append(lambda: sent_units(buf_a, ha_s))
    out_units(1 + OUT[0], OUT[1])
    next_out = 1 + OUT[0] + OUT[1]

    def share(u):
        def pack(q, carry):
            pax[u, q] = acc[u, 2 * q + 1 - c]
            return carry

        lax.fori_loop(0, 4, pack, 0)
        return send(pax.at[u], prx.at[u], px_s.at[u], px_r.at[u], partner)

    def summed(u, q):
        return acc[u, 2 * q + c] + prx[u, q]

    total = jnp.zeros((128, quarter), F32)
    for g in range(4):
        landed(hret.at[pl.ds(g * 16, 16)], ha_r.at[g])
        total = total + mm(c01[:, g * 256 : (g + 1) * 256], hret[g * 16 : (g + 1) * 16].reshape(256, quarter))
    acc[0] = total.reshape(8, 16, quarter)
    sh0 = share(0)
    sh0.wait_recv()
    pending.append(sh0.wait_send)

    dots = jnp.zeros((16, 1), F32)
    for q in range(4):
        cols = slice(q * quarter, (q + 1) * quarter)
        scaled = summed(0, q) * gain[:, cols].astype(F32)
        dots = dots + jnp.sum(scaled * (stream[:, cols].astype(F32) * inverse), axis=1, keepdims=True)
    mean = dots / width
    for q in range(4):
        cols = slice(q * quarter, (q + 1) * quarter)
        scaled = summed(0, q) * gain[:, cols].astype(F32)
        unit = stream[:, cols].astype(F32) * inverse
        gs_o[:, cols] = (cot[:, cols].astype(F32) + inverse * (scaled - unit * mean)).astype(BF)

    for m in range(4):
        for h in range(2):
            at = (4 * h + m) * half
            gsp[m, :, h * half : (h + 1) * half] = gs_o[:, at : at + half]
    for k in (2, 1, 3):
        to = (z + k) % 4
        pending.append(send(gsp.at[to], gs_all.at[tn, z], gx_s.at[k], gx_r.at[z], over_z[k]).wait_send)
    pltpu.make_async_copy(gsp.at[z], gs_all.at[tn, z], gx_r.at[z]).start()
    out_units(next_out, OUT[2])
    next_out2 = next_out + OUT[2]
    next_out2 = next_out + OUT[2]
    for n, k in enumerate((1, 3, 2, 0)):
        m = (z + k) % 4
        landed(gs_all.at[tn, m], gx_r.at[m])

        def gather_gs(i, carry):
            t2 = ((tc // 4 + i // 4) % 2) * 4 + (y + i % 4) % 4
            send(gs_all.at[tn, m], gs_all.at[tn, m], gs_s.at[m], gs_r.at[m, tc], (dp, t2 * 2 + c))
            return carry

        lax.fori_loop(1, 8, gather_gs, 0)
        send(gs_all.at[tn, m], gs_all.at[tn, m], fw_s.at[m], fw_r.at[m, tc], partner)
        out_units(next_out2 + n * OUT[3], OUT[3])

    for k in (1, 3, 2, 0):
        m = (z + k) % 4

        def forward_gs(i, carry):
            t2 = ((tc // 4 + i // 4) % 2) * 4 + (y + i % 4) % 4
            b2 = t2 * 2 + c
            landed(gs_all.at[b2, m], gs_r.at[m, t2])
            send(gs_all.at[b2, m], gs_all.at[b2, m], fw_s.at[m], fw_r.at[m, t2], partner)
            return carry

        lax.fori_loop(1, 8, forward_gs, 0)

        def all_gs(t, carry):
            landed(gs_all.at[t * 2 + 1 - c, m], fw_r.at[m, t])
            return carry

        lax.fori_loop(0, 8, all_gs, 0)
        gh = mm_t(down2[...], gs_all[:, m].reshape(256, quarter))
        if k:
            ghs[k] = gh.astype(BF)
            pending.append(send(ghs.at[k], ghr.at[z], gh_s.at[k], gh_r.at[z], over_z[k]).wait_send)

    def gs_sent():
        for m in range(4):
            landed(gs_all.at[pl.ds(0, 7), 0], gs_s.at[m])
            landed(gs_all.at[pl.ds(0, 8), 0], fw_s.at[m])

    pending.append(gs_sent)
    return_units(buf_b, eret, ea_s, ea_r, next_out2 + 4 * OUT[3])
    pending.append(lambda: sent_units(buf_b, ea_s))

    total = jnp.zeros((256, quarter), F32)
    for g in range(4):
        landed(eret.at[pl.ds(g * 16, 16)], ea_r.at[g])
        total = total + mm(cw[:, g * 256 : (g + 1) * 256], eret[g * 16 : (g + 1) * 16].reshape(256, quarter))
    acc[1] = (total[0:128] + total[128:256]).reshape(8, 16, quarter)
    sh1 = share(1)
    sh1.wait_recv()
    pending.append(sh1.wait_send)
    for q in range(4):
        cols = slice(q * quarter, (q + 1) * quarter)
        moe_o[:, cols] = (stream[:, cols].astype(F32) + summed(1, q)).astype(BF)

    for k in (1, 3, 2):
        at = (z + k) % 4
        landed(ghr.at[at], gh_r.at[at])
        gh = gh + ghr[at].astype(F32)
    gh_o[...] = gh.astype(BF)

    drain()


def hand_over(a, b, c, a_o, b_o, c_o):
    a_o[...] = a[...]
    b_o[...] = b[...]
    c_o[...] = c[...]


def body(
    dense_hidden, dense_down, residual, norm_gain, expert_ids, route_weights,
    w_gate, w_up, w_down, out_cotangent,
):
    width = residual.shape[1]
    q = width // 4
    hidden_units, cols = dense_down.shape
    fe = w_gate.shape[2]

    vmem = pl.BlockSpec(memory_space=pltpu.VMEM)
    hbm = pl.BlockSpec(memory_space=pl.ANY)
    V = pltpu.VMEM
    dma = pltpu.SemaphoreType.DMA
    unit = (CHIPS, ROWS, q)
    scratch = [
        V((4, hidden_units, 256), BF), V((2 * cols, hidden_units), BF), V((hidden_units, q), BF),
        V((width, fe), BF), V((width, fe), BF), V((fe, width), BF),
        V((1, width), BF), V((2, 16, width), BF), V((2, 8, 128), F32), V((2, 8, 128), F32), V((2, 16, width), BF),
        V((1024, 128), BF), V((1024, 256), BF), V((128, 1024), BF), V((256, 1024), BF),
        V((256, 256), BF), V((256, 256), BF), V((128, q), BF), V((256, q), BF),
        V(unit, BF), V(unit, BF), V(unit, BF), V(unit, BF), V(unit, BF), V(unit, BF),
        V((256, width), BF), V((256, fe), F32), V((256, fe), F32), V((256, fe), BF), V((256, fe), BF), V((256, fe), BF),
        V((4, 256, q), BF),
        V((4, 16, 16, q), F32), V((4, 8, 16, q), BF), V((4, 8, 16, q), BF), V((4, 8, 16, q), BF),
        V((4, 8, 16, q), BF), V((4, 16, q), F32), V((4, 16, q), F32), V((16, width), F32), V((16, width), BF),
        V((2, 8, 16, q), F32), V((2, 4, 16, q), F32), V((2, 4, 16, q), F32), V((4, 16, q), BF), V((16, 4, 16, q), BF),
        V((4, hidden_units, 256), BF), V((4, hidden_units, 256), BF),
        pltpu.SemaphoreType.REGULAR, pltpu.SemaphoreType.REGULAR,
        dma((4,)), dma((4,)), dma((4,)), dma((4,)), dma((4,)), dma, dma((2,)), dma((4,)), dma((4,)), dma((4,)), dma((4,)), dma((4,)), dma((4,)), dma((4,)), dma((4,)), dma((4,)), dma((4,)),
        dma, dma((4,)), dma, dma((4,)), dma, dma((4,)), dma, dma((4,)),
        dma((2,)), dma((2,)), dma((4,)), dma((4, 8)), dma((4,)), dma((4, 8)),
    ]
    moe, gs, gh = pl.pallas_call(
        kernel,
        out_shape=(
            jax.ShapeDtypeStruct(residual.shape, BF),
            jax.ShapeDtypeStruct(residual.shape, BF),
            jax.ShapeDtypeStruct(dense_hidden.shape[::-1], BF),
        ),
        in_specs=[hbm, hbm, vmem, vmem, vmem, vmem, vmem, hbm, hbm, hbm],
        out_specs=(vmem, vmem, vmem),
        scratch_shapes=scratch,
        compiler_params=pltpu.CompilerParams(
            collective_id=0, has_side_effects=True, vmem_limit_bytes=63 * 1024 * 1024
        ),
    )(
        dense_hidden.T, dense_down.T, residual, norm_gain, out_cotangent, expert_ids.T, route_weights.T,
        w_gate[0], w_up[0], w_down[0],
    )
    moe, gs, gh = pl.pallas_call(
        hand_over,
        out_shape=tuple(jax.ShapeDtypeStruct(a.shape, a.dtype) for a in (moe, gs, gh)),
        in_specs=[vmem] * 3,
        out_specs=(vmem,) * 3,
    )(moe, gs, gh)
    return moe, gs, gh.T


def solution(mesh):
    rows = P(("dp", "tensor"), None)
    experts = P(("dp", "tensor"), None, None)
    placed = (P("dp", "tensor"), P("tensor", "dp"), rows, P(), rows, rows, experts, experts, experts, rows)
    return jax.shard_map(
        body, mesh=mesh, in_specs=placed, out_specs=(rows, rows, P("dp", "tensor")), check_vma=False
    )
```
